128 devices in a mesh: tok: 32 (over z, y, x_hi), row: 2 (over x_lo), col: 2 (over core).
Axes of the slice: x: 4 (x_hi: 2, x_lo: 2; x = x_hi * 2 + x_lo), y: 4, z: 4, core: 2. Of those that a mesh axis runs over, the one named last changes fastest.
Arguments:
- tokens: bfloat16 [960, 16384], P('row', ('tok', 'col')), may hold values from -6 to 6
- gain_attn: float32 [960], P('row'), may hold values from 0.5 to 1.5
- gain_mlp: float32 [960], P('row'), may hold values from 0.5 to 1.5
- w_query: bfloat16 [960, 960], P('row', 'col'), may hold values from -0.1875 to 0.1875
- w_key: bfloat16 [960, 320], P('row', 'col'), may hold values from -0.1875 to 0.1875
- w_value: bfloat16 [960, 320], P('row', 'col'), may hold values from -0.1875 to 0.1875
- w_out: bfloat16 [960, 960], P('col', 'row'), may hold values from -0.75 to 0.75
- w_gate: bfloat16 [960, 2560], P('row', 'col'), may hold values from -0.1875 to 0.1875
- w_up: bfloat16 [960, 2560], P('row', 'col'), may hold values from -0.1875 to 0.1875
- w_down: bfloat16 [960, 2560], P('row', 'col'), may hold values from -0.25 to 0.25
- seq_lengths: int32 [128, 3], P(('tok', 'row', 'col')), may hold values from 1 to 96, 128 in all within a row
- cotangent: float32 [960, 16384], P('row', ('tok', 'col')), may hold values from -6 to 6
Outputs:
- output: float32 [960, 16384], P('row', ('tok', 'col'))
- grad_tokens: float32 [960, 16384], P('row', ('tok', 'col'))
- grad_gain_attn: float32 [960], P('row')
- grad_gain_mlp: float32 [960], P('row')
- grad_w_query: float32 [960, 960], P('row', 'col')
- grad_w_key: float32 [960, 320], P('row', 'col')
- grad_w_value: float32 [960, 320], P('row', 'col')
- grad_w_out: float32 [960, 960], P('col', 'row')
- grad_w_gate: float32 [960, 2560], P('row', 'col')
- grad_w_up: float32 [960, 2560], P('row', 'col')
- grad_w_down: float32 [960, 2560], P('row', 'col')
The draws below stay inside these ranges and needn't reach their ends.
Inputs may be any that keep to these rules, and one draw needn't show every extreme that they name: `seq_lengths`: row s holds the lengths of the 3 sequences of token shard s in order; each row sums to 128 and its largest entry is exactly 96.
All inputs are finite; a program needn't handle non-finite values.
Results may differ from the reference program's by a relative error of at most 0.025.
Values may be sent and summed in bfloat16 or wider, within the bound.
A program may use at most 128 MiB of HBM per device.

```python
import math
import jax
import jax.numpy as jnp
import numpy as np
from jax import lax

D = 960
HQ = 15
KVH = 5
HD = 64
FF = 2560
TOK_DEV = 128
SEQ_DEV = 3
LONGEST = 96
TOKENS = 16384
SHARDS = 128


def level_of(stream_key, extent, cuts, smallest, high):
    def one(axis_at, parts):
        draws = jax.random.uniform(jax.random.fold_in(jax.random.fold_in(stream_key, 6), axis_at), (parts,), jnp.float32, smallest / len(cuts), high / len(cuts))
        return jnp.repeat(jnp.exp(draws), extent[axis_at] // parts).reshape((-1,) + (1,) * (len(extent) - axis_at - 1))

    factor_of = one(*cuts[0])
    for cut in cuts[1:]:
        factor_of = factor_of * one(*cut)
    return factor_of


def length_profile(count, total, bound, slope):
    weights = [(1 << 20) // math.isqrt(grade ** slope) + 1 for grade in range(2, count + 1)]
    rest, given = total - bound - (count - 1), [1] * (count - 1)
    while rest > 0:
        free = [i for i in range(count - 1) if given[i] < bound]
        whole, budget = sum([weights[i] for i in free]), rest
        for i in free:
            addition = min(bound - given[i], max(1, budget * weights[i] // whole), rest)
            given[i] = given[i] + addition
            rest = rest - addition
    return np.array([bound] + given)


def ragged(stream_key, count, total, most, lean):
    if count == 2:
        one = jax.random.randint(stream_key, (), max(1, total - most), min(most, total - 1) + 1)
        return jnp.stack([one, total - one])
    sizes = jnp.asarray(length_profile(count, total, most, lean), jnp.int32)
    twos = (count - 1) // 2
    donor, sink = sizes[1:1 + 2 * twos:2], sizes[2:2 + 2 * twos:2]
    room = jnp.minimum(donor - 1, most - sink)
    shifted = jax.random.randint(jax.random.fold_in(stream_key, 1), (twos,), 0, 1 << 20) % (room + 1)
    sizes = sizes.at[1:1 + 2 * twos:2].set(donor - shifted).at[2:2 + 2 * twos:2].set(sink + shifted)
    return sizes[jax.random.permutation(jax.random.fold_in(stream_key, 2), count)]


def centred(key, shape, spread, bound, pieces=(), held_as=jnp.bfloat16):
    values = jax.random.normal(key, shape, jnp.float32) * spread
    if len(pieces) > 0:
        values = level_of(key, shape, pieces, -0.22, 0.18) * values
    return jnp.clip(values, min=-bound, max=bound).astype(held_as)


def setup_inputs(seed: int = 0) -> dict:
    key_list = jax.random.split(jax.random.key(seed), 13)
    tokens = centred(key_list[0], (D, TOKENS), 1.0, 6.0, ((0, 2), (1, 64)))
    gain_attn = jnp.clip(1.0 + 0.1 * jax.random.normal(key_list[1], (D,), jnp.float32), 0.5, 1.5)
    gain_mlp = jnp.clip(1.0 + 0.1 * jax.random.normal(key_list[2], (D,), jnp.float32), 0.5, 1.5)
    w_query = centred(key_list[3], (D, HQ * HD), D ** -0.5, 0.1875, ((0, 2), (1, 2)))
    w_key = centred(key_list[4], (D, KVH * HD), D ** -0.5, 0.1875, ((0, 2), (1, 2)))
    w_value = centred(key_list[5], (D, KVH * HD), D ** -0.5, 0.1875, ((0, 2), (1, 2)))
    w_out = centred(key_list[6], (HQ * HD, D), (HQ * HD // 16) ** -0.5, 0.75, ((0, 2), (1, 2)))
    w_gate = centred(key_list[7], (D, FF), D ** -0.5, 0.1875, ((0, 2), (1, 2)))
    w_up = centred(key_list[8], (D, FF), D ** -0.5, 0.1875, ((0, 2), (1, 2)))
    w_down = centred(key_list[9], (D, FF), (FF // 4) ** -0.5, 0.25, ((0, 2), (1, 2)))
    seq_lengths = jax.vmap(lambda own: ragged(own, SEQ_DEV, TOK_DEV, LONGEST, 2))(jax.random.split(key_list[10], SHARDS)).reshape((SHARDS, SEQ_DEV)).astype(jnp.int32)
    cotangent = centred(key_list[11], (D, TOKENS), 1.0, 6.0, ((0, 2), (1, 64)), jnp.float32)
    return dict(tokens=tokens, gain_attn=gain_attn, gain_mlp=gain_mlp, w_query=w_query, w_key=w_key, w_value=w_value, w_out=w_out, w_gate=w_gate, w_up=w_up, w_down=w_down, seq_lengths=seq_lengths, cotangent=cotangent)


EPS = 1e-05
THETA = 100000.0

@jax.custom_vjp
def low(v):
    return lax.optimization_barrier(v.astype(jnp.bfloat16)).astype(jnp.float32)

@jax.custom_vjp
def low_back(v):
    return v

def low_keep(v):
    return (low(v), None)

def low_pass(kept, grad):
    return (grad,)

def back_keep(v):
    return (v, None)

def back_low(kept, grad):
    return (low(grad),)
low.defvjp(low_keep, low_pass)
low_back.defvjp(back_keep, back_low)

def matmul(left, right):
    return jnp.dot(left, right, precision=lax.Precision.HIGHEST, preferred_element_type=jnp.float32)

def rms_norm(resid, gain):
    scale = lax.rsqrt(lax.optimization_barrier(jnp.mean(resid * resid, axis=1, keepdims=True)) + EPS)
    return resid * scale * gain

def tables(seq_lengths):
    ends = jnp.cumsum(seq_lengths, axis=1).astype(jnp.int32)
    starts = (ends - seq_lengths).astype(jnp.int32)
    index = jnp.arange(TOK_DEV, dtype=jnp.int32)
    segment = lax.optimization_barrier(jnp.sum((index[None, :, None] >= ends[:, None, :]).astype(jnp.int32), axis=2))
    onehot = segment[:, :, None] == jnp.arange(SEQ_DEV, dtype=jnp.int32)[None, None, :]
    begin = lax.optimization_barrier(jnp.sum(jnp.where(onehot, starts[:, None, :], 0), axis=2))
    place = (index[None, :] - begin).astype(jnp.float32)
    freq = jnp.exp(jnp.arange(0, HD, 2, dtype=jnp.float32) * (-math.log(THETA) / HD))
    angle = place[:, :, None] * freq[None, None, :]
    return (segment, jnp.cos(angle), jnp.sin(angle))

def rotate(value, cosine, sine):
    half = value.shape[-1] // 2
    first = value[..., :half]
    second = value[..., half:]
    cos_b = cosine[:, :, None, :]
    sin_b = sine[:, :, None, :]
    return jnp.concatenate([first * cos_b - second * sin_b, second * cos_b + first * sin_b], axis=-1)

def attend(block):
    query, key, value, segment = block
    grouped = query.reshape(TOK_DEV, KVH, HQ // KVH, HD)
    raw = jnp.einsum('qhgd,khd->hgqk', grouped, key, precision=lax.Precision.HIGHEST)
    scores = low_back(raw * HD ** (-0.5))
    index = jnp.arange(TOK_DEV, dtype=jnp.int32)
    allowed = (segment[:, None] == segment[None, :]) & (index[None, :] <= index[:, None])
    probs = low(jax.nn.softmax(jnp.where(allowed, scores, -1e+30), axis=-1))
    context = jnp.einsum('hgqk,khd->qhgd', probs, value, precision=lax.Precision.HIGHEST)
    return context.reshape(TOK_DEV, HQ * HD)

def layer(tokens_t, gain_attn, gain_mlp, w_query, w_key, w_value, w_out, w_gate, w_up, w_down_t, segment, cosine, sine):
    resid = tokens_t.T
    normed_one = low(rms_norm(resid, gain_attn))
    query = low_back(matmul(normed_one, w_query))
    key = low_back(matmul(normed_one, w_key))
    value = low(low_back(matmul(normed_one, w_value)))
    query = low(rotate(query.reshape(SHARDS, TOK_DEV, HQ, HD), cosine, sine))
    key = low(rotate(key.reshape(SHARDS, TOK_DEV, KVH, HD), cosine, sine))
    value = value.reshape(SHARDS, TOK_DEV, KVH, HD)
    context = lax.map(jax.checkpoint(attend), (query, key, value, segment))
    context = low(low_back(context.reshape(TOKENS, HQ * HD)))
    mid = resid + low_back(matmul(context, w_out))
    normed_two = low(rms_norm(mid, gain_mlp))
    gate = low_back(matmul(normed_two, w_gate))
    up = low_back(matmul(normed_two, w_up))
    hidden = low(jax.nn.silu(gate) * up)
    return (mid + low_back(matmul(hidden, w_down_t.T))).T

def reference(tokens, gain_attn, gain_mlp, w_query, w_key, w_value, w_out, w_gate, w_up, w_down, seq_lengths, cotangent):
    segment, cosine, sine = tables(seq_lengths)

    def forward(*params):
        return layer(*params, segment, cosine, sine)
    params = (tokens.astype(jnp.float32), gain_attn, gain_mlp, w_query.astype(jnp.float32), w_key.astype(jnp.float32), w_value.astype(jnp.float32), w_out.astype(jnp.float32), w_gate.astype(jnp.float32), w_up.astype(jnp.float32), w_down.astype(jnp.float32))
    output, pullback = jax.vjp(forward, *params)
    grads = pullback(cotangent)
    return (output, grads[0], grads[1], grads[2], grads[3], grads[4], grads[5], grads[6], grads[7], grads[8], grads[9])
```

```python
import math

import jax
import jax.numpy as jnp
from jax import lax
from jax.experimental import pallas as pl
from jax.experimental.pallas import tpu as pltpu
from jax.sharding import PartitionSpec as P

MESH = pl.DeviceIdType.MESH
MIB = 1024 * 1024


def position():
    t = lax.axis_index("tok")
    r = lax.axis_index("row")
    c = lax.axis_index("col")
    return {"x": (t % 2) * 2 + r, "y": (t // 2) % 4, "z": t // 8, "c": c}


def device(place, axis, step):
    p = dict(place)
    p[axis] = (p[axis] + step) % (2 if axis == "c" else 4)
    return (p["z"] * 8 + p["y"] * 2 + p["x"] // 2, p["x"] % 2, p["c"])


def meet(place):
    barrier = pltpu.get_barrier_semaphore()
    partners = [("c", 1)] + [(a, d) for a in "xyz" for d in (1, 2, 3)]
    for axis, step in partners:
        pl.semaphore_signal(
            barrier, inc=1, device_id=device(place, axis, step), device_id_type=MESH
        )
    pl.semaphore_wait(barrier, len(partners))


def send(src, dst, send_sem, recv_sem, target):
    copy = pltpu.make_async_remote_copy(
        src_ref=src, dst_ref=dst, send_sem=send_sem, recv_sem=recv_sem,
        device_id=target, device_id_type=MESH,
    )
    copy.start()
    return copy


ROWS = 512
STREAMS = (
    ("down", 1280, "xyz"),
    ("gate", 1280, "yzx"),
    ("up", 1280, "zxy"),
    ("out", 480, "xyz"),
    ("q", 480, "yzx"),
    ("kv", 384, "zxy"),
)


def aligned(value, unit):
    return pl.multiple_of(value, unit)


class Stream:
    def __init__(self, order, place):
        self.order = order
        self.place = place

    def piece(self, acc, level, owner):
        size, start, lead = ROWS, 0, None
        for depth in range(level + 1):
            axis = self.order[depth]
            index = owner if depth == level else self.place[axis]
            if axis == "x":
                size //= 2
                start = start + (index // 2) * size
                lead = index % 2
            else:
                size //= 4
                start = start + index * size
        rows = pl.ds(aligned(start, 16), size)
        if lead is None:
            return acc.at[:, rows]
        return acc.at[lead, rows]

    def result(self, out, level):
        size, start = ROWS, 0
        for depth in range(level + 1):
            axis = self.order[depth]
            size //= 2 if axis == "x" else 4
            start = start + (self.place[axis] // 2 if axis == "x" else self.place[axis]) * size
        return out.at[pl.ds(aligned(start, 16), size)]

    def shape(self, level, n):
        size, lead = ROWS, 2
        for depth in range(level + 1):
            if self.order[depth] == "x":
                size //= 2
                lead = 1
            else:
                size //= 4
        return (lead, size, n) if lead == 2 else (size, n)


def add_rows(dst, srcs, step=16):
    shape = dst.shape
    if len(shape) == 2:
        views = [(dst, srcs)]
    else:
        views = [(dst.at[k], [s.at[k] for s in srcs]) for k in range(shape[0])]
    rows = shape[-2]
    step = min(step, rows)
    for d, ss in views:
        @pl.loop(0, rows // step)
        def _(i, d=d, ss=ss):
            at = pl.ds(aligned(i * step, step), step)
            total = d[at, :].astype(jnp.float32)
            for s in ss:
                total = total + s[at, :].astype(jnp.float32)
            d[at, :] = total.astype(d.dtype)


def reduce_kernel(*refs):
    k = len(STREAMS)
    src = refs[:k]
    out = refs[k : 2 * k]
    scr = list(refs[2 * k :])
    acc, mate = scr[:k], scr[k : 2 * k]
    got = [scr[2 * k + 3 * i : 2 * k + 3 * i + 3] for i in range(k)]
    load_sem, mate_send, mate_recv, rs_send, rs_recv, ag_send, ag_recv = scr[5 * k :]
    place = position()
    c = place["c"]
    meet(place)
    streams = [Stream(order, place) for _, _, order in STREAMS]
    loads, mates = [], []
    for i in range(k):
        mates.append(
            send(src[i].at[1 - c], mate[i], mate_send.at[i], mate_recv.at[i], device(place, "c", 1))
        )
        load = pltpu.make_async_copy(src[i].at[c], acc[i], load_sem.at[i])
        load.start()
        loads.append(load)
    pending = []

    def scatter(i, level):
        axis = streams[i].order[level]
        copies = []
        for d in (2, 1, 3):
            slot = got[i][level].at[d - 1]
            copies.append(
                send(
                    streams[i].piece(acc[i], level, (place[axis] + d) % 4), slot,
                    rs_send.at[i, level, d - 1], rs_recv.at[i, level, d - 1], device(place, axis, d),
                )
            )
        return copies

    def gather(i, level):
        axis = streams[i].order[level]
        copies = []
        part = streams[i].result(out[i], level)
        for d in (2,) if axis == "x" else (2, 1, 3):
            copies.append(
                send(part, part, ag_send.at[i, level, d - 1], ag_recv.at[i, level, d - 1], device(place, axis, d))
            )
        return copies

    flying = {}
    for phase in range(7):
        for i in range(k):
            if phase == 0:
                loads[i].wait()
                mates[i].wait_recv()
                for lead in range(2):
                    add_rows(acc[i].at[lead], [mate[i].at[lead]])
                flying[i] = scatter(i, 0)
            elif phase <= 3:
                level = phase - 1
                for copy in flying[i]:
                    copy.wait()
                mine = streams[i].piece(acc[i], level, place[streams[i].order[level]])
                add_rows(mine, [got[i][level].at[d] for d in range(3)])
                if level < 2:
                    flying[i] = scatter(i, level + 1)
                else:
                    streams[i].result(out[i], 2)[...] = mine[...]
                    flying[i] = gather(i, 2)
            else:
                for copy in flying[i]:
                    copy.wait()
                level = 5 - phase
                if level >= 0:
                    flying[i] = gather(i, level)
    for i in range(k):
        mates[i].wait_send()


def reduce_grads(grads):
    k = len(STREAMS)
    place = {"x": 0, "y": 0, "z": 0, "c": 0}
    scratch = [pltpu.VMEM((2, ROWS, n), jnp.bfloat16) for _, n, _ in STREAMS] * 2
    for _, n, order in STREAMS:
        for level in range(3):
            scratch.append(
                pltpu.VMEM((3,) + Stream(order, place).shape(level, n), jnp.bfloat16)
            )
    dma = pltpu.SemaphoreType.DMA
    scratch += [dma((k,)), dma((k,)), dma((k,)), dma((k, 3, 3)), dma((k, 3, 3)), dma((k, 3, 3)), dma((k, 3, 3))]
    return pl.pallas_call(
        reduce_kernel,
        out_shape=[jax.ShapeDtypeStruct((ROWS, n), jnp.bfloat16) for _, n, _ in STREAMS],
        in_specs=[pl.BlockSpec(memory_space=pl.ANY)] * k,
        out_specs=[pl.BlockSpec(memory_space=pltpu.VMEM)] * k,
        scratch_shapes=scratch,
        compiler_params=pltpu.CompilerParams(
            collective_id=1, has_side_effects=True, vmem_limit_bytes=56 * MIB
        ),
        cost_estimate=pl.CostEstimate(flops=0, bytes_accessed=60 * MIB, transcendentals=0),
    )(*grads)

UNIT = 48


def gather_kernel(*refs):
    k = 5
    src, (tok, cot, seq) = refs[:k], refs[k : k + 3]
    full = refs[k + 3 : 2 * k + 3]
    tok_all, cot_all, seq_own = refs[2 * k + 3 : 2 * k + 6]
    seq_in, local_sem, x_send, x_recv, relay_send, relay_recv, mate_send, mate_recv, act_send, act_recv = refs[2 * k + 6 :]
    place = position()
    r, c = place["x"] % 2, place["c"]
    t = lax.axis_index("tok")
    barrier = pltpu.get_barrier_semaphore()
    partners = [device(place, "c", 1)]
    partners += [device(place, a, d) for a in "xyz" for d in ((1, 3) if a == "x" else (1, 2, 3))]
    partners.append((t, 1 - r, 1 - c))
    for target in partners:
        pl.semaphore_signal(barrier, inc=1, device_id=target, device_id_type=MESH)
    pl.semaphore_wait(barrier, len(partners))

    def rows(unit):
        return pl.ds(aligned(unit * UNIT, 16), UNIT)

    row_mate = (t, 1 - r, c)
    waits, locals_ = [], []
    x_in = []
    for i in range(k):
        own, there = src[i], full[i].at[r, c]
        arrive = []
        for j, (step, unit) in enumerate(((1, place["y"]), (3, 4 + place["z"]), (1, 8), (3, 9))):
            copy = send(
                own.at[rows(unit)], there.at[rows(unit)], x_send.at[i, j], x_recv.at[i, j],
                device(place, "x", step),
            )
            arrive.append(copy)
            waits.append(copy)
        x_in.append(arrive)
        if i == 0:
            seq_copy = send(seq, seq_in, act_send.at[2], act_recv.at[2], (t, 1 - r, 1 - c))
            theirs = pl.ds(aligned((1 - r) * 128, 128), 128)
            tok_copy = send(tok.at[:, theirs], tok_all.at[r], act_send.at[0], act_recv.at[0], row_mate)
    cot_copy = send(cot.at[:, theirs], cot_all.at[r], act_send.at[1], act_recv.at[1], row_mate)
    own_mate = []
    for i in range(k):
        copy = send(src[i], full[i].at[r, c], mate_send.at[i, 0], mate_recv.at[i, 0], device(place, "c", 1))
        own_mate.append(copy)
        local = pltpu.make_async_copy(src[i], full[i].at[r, c], local_sem.at[i])
        local.start()
        locals_.append(local)
    mine = pl.ds(aligned(r * 128, 128), 128)
    for j, (a, b) in enumerate(((tok.at[:, mine], tok_all.at[r]), (cot.at[:, mine], cot_all.at[r]))):
        local = pltpu.make_async_copy(a, b, local_sem.at[k + j])
        local.start()
        locals_.append(local)
    relays = []
    for i in range(k):
        there = full[i].at[1 - r, c]
        relay = []
        for j, (axis, unit) in enumerate((("y", place["y"]), ("z", 4 + place["z"]))):
            x_in[i][j].wait_recv()
            for d in (2, 1, 3):
                copy = send(
                    there.at[rows(unit)], there.at[rows(unit)], relay_send.at[i, j, d - 1],
                    relay_recv.at[i, j, d - 1], device(place, axis, d),
                )
                relay.append(copy)
        relays.append(relay)
    forwards = []
    for i in range(k):
        there = full[i].at[1 - r, c]
        for copy in x_in[i][2:] + []:
            copy.wait_recv()
        for copy in relays[i]:
            copy.wait_recv()
        forwards.append(
            send(there, there, mate_send.at[i, 1], mate_recv.at[i, 1], device(place, "c", 1))
        )
    seq_copy.wait()
    seq_own[...] = jnp.where(r == c, seq[...], seq_in[...])
    for copy in locals_ + own_mate + forwards + [tok_copy, cot_copy]:
        copy.wait()
    for copy in waits:
        copy.wait_send()
    for relay in relays:
        for copy in relay:
            copy.wait_send()


def gather_weights(weights, tokens, cotangent, seq):
    k = len(weights)
    hbm, vmem = pl.BlockSpec(memory_space=pl.ANY), pl.BlockSpec(memory_space=pltpu.VMEM)
    dma = pltpu.SemaphoreType.DMA
    return pl.pallas_call(
        gather_kernel,
        out_shape=[jax.ShapeDtypeStruct((2, 2) + w.shape, w.dtype) for w in weights]
        + [
            jax.ShapeDtypeStruct((2, 480, 128), tokens.dtype),
            jax.ShapeDtypeStruct((2, 480, 128), cotangent.dtype),
            jax.ShapeDtypeStruct((8, 128), jnp.int32),
        ],
        in_specs=[hbm] * (k + 2) + [vmem],
        out_specs=[vmem] * (k + 3),
        scratch_shapes=[
            pltpu.VMEM((8, 128), jnp.int32), dma((k + 2,)), dma((k, 4)), dma((k, 4)), dma((k, 2, 3)),
            dma((k, 2, 3)), dma((k, 2)), dma((k, 2)), dma((3,)), dma((3,)),
        ],
        compiler_params=pltpu.CompilerParams(collective_id=2, has_side_effects=True, vmem_limit_bytes=48 * MIB),
        cost_estimate=pl.CostEstimate(flops=0, bytes_accessed=40 * MIB, transcendentals=0),
    )(*weights, tokens, cotangent, seq)

D = 960
HQ = 15
KVH = 5
HD = 64
EPS = 1e-05
THETA = 100000.0


def nn(left, right):
    return jnp.dot(left, right, preferred_element_type=jnp.float32)


def nt(left, right):
    return lax.dot_general(
        left, right, (((1,), (1,)), ((), ())), preferred_element_type=jnp.float32
    )


def low(value):
    return value.astype(jnp.bfloat16)


def tables(seq):
    first, second = seq[0:1, 0:1], seq[0:1, 0:1] + seq[0:1, 1:2]

    def segment(index):
        return (index >= first).astype(jnp.int32) + (index >= second).astype(jnp.int32)

    lane = lax.broadcasted_iota(jnp.int32, (1, 128), 1)
    seg_q = segment(lane)
    begin = jnp.where(seg_q == 0, 0, jnp.where(seg_q == 1, first, second))
    place = (lane - begin).astype(jnp.float32)
    ladder = lax.broadcasted_iota(jnp.int32, (32, 128), 0).astype(jnp.float32)
    angle = place * jnp.exp(ladder * (-2.0 * math.log(THETA) / HD))
    rows = lax.broadcasted_iota(jnp.int32, (128, 128), 0)
    lanes = lax.broadcasted_iota(jnp.int32, (128, 128), 1)
    seg_rows = (rows >= first).astype(jnp.int32) + (rows >= second).astype(jnp.int32)
    seg_lanes = (lanes >= first).astype(jnp.int32) + (lanes >= second).astype(jnp.int32)
    allowed = (seg_rows == seg_lanes) & (rows <= lanes)
    return jnp.cos(angle), jnp.sin(angle), allowed


def rotate(head, cosine, sine):
    a, b = head[:32], head[32:]
    return jnp.concatenate([a * cosine - b * sine, b * cosine + a * sine], axis=0)


def features_total(parts):
    return jnp.sum(parts[0], axis=0, keepdims=True) + jnp.sum(parts[1], axis=0, keepdims=True)


def inverse_rms(parts):
    return lax.rsqrt(features_total([p * p for p in parts]) / D + EPS)


def norm_back(resid, scale, gain, grad):
    weighted = [grad[r] * gain[r] for r in range(2)]
    inner = features_total([weighted[r] * resid[r] for r in range(2)]) / D
    grad_resid = [
        weighted[r] * scale - resid[r] * (scale * scale * scale * inner) for r in range(2)
    ]
    grad_gain = [jnp.sum(grad[r] * resid[r] * scale, axis=1, keepdims=True) for r in range(2)]
    return grad_resid, grad_gain


def layer(w_qkv, w_out, w_gate, w_up, w_down, tok, cot, seq, gain_one, gain_two):
    two = range(2)
    cosine, sine, allowed = tables(seq)
    resid = [tok[r].astype(jnp.float32) for r in two]
    scale_one = inverse_rms(resid)
    n1t = [low(resid[r] * scale_one * gain_one[r]) for r in two]
    n1 = [n.T for n in n1t]
    qkv = [(nn(n1[0], w_qkv[0, c]) + nn(n1[1], w_qkv[1, c])).T for c in two]
    q = jnp.concatenate([qkv[0][:480], qkv[1][:480]], axis=0)
    k = jnp.concatenate([qkv[0][480:640], qkv[1][480:640]], axis=0)
    v = low(jnp.concatenate([qkv[0][640:], qkv[1][640:]], axis=0))
    heads = []
    ctx = []
    mask = jnp.concatenate([allowed] * 3, axis=1)
    for h in range(KVH):
        kt = low(rotate(k[h * 64 : h * 64 + 64], cosine, sine))
        vt = v[h * 64 : h * 64 + 64]
        qcat = jnp.concatenate(
            [low(rotate(q[j * 64 : j * 64 + 64], cosine, sine)) for j in range(3 * h, 3 * h + 3)], axis=1
        )
        scores = jnp.where(mask, nn(kt.T, qcat) * HD ** (-0.5), -1e30)
        expo = jnp.exp(scores - jnp.max(scores, axis=0, keepdims=True))
        probs = expo / jnp.sum(expo, axis=0, keepdims=True)
        out = low(nn(vt, low(probs)))
        ctx += [out[:, j * 128 : j * 128 + 128] for j in range(3)]
        heads.append((kt, vt, qcat, probs))
    ctx = jnp.concatenate(ctx, axis=0)
    ctxt = [ctx[:480], ctx[480:]]
    ctxn = [x.T for x in ctxt]
    mid = [
        resid[r] + (nn(ctxn[0], w_out[r, 0]) + nn(ctxn[1], w_out[r, 1])).T for r in two
    ]
    scale_two = inverse_rms(mid)
    n2t = [low(mid[r] * scale_two * gain_two[r]) for r in two]
    n2 = [n.T for n in n2t]
    gate = [nn(n2[0], w_gate[0, c]) + nn(n2[1], w_gate[1, c]) for c in two]
    up = [nn(n2[0], w_up[0, c]) + nn(n2[1], w_up[1, c]) for c in two]
    sig = [jax.nn.sigmoid(g) for g in gate]
    silu = [gate[c] * sig[c] for c in two]
    hidden = [low(silu[c] * up[c]) for c in two]
    out = [mid[r] + nt(w_down[r, 0], hidden[0]) + nt(w_down[r, 1], hidden[1]) for r in two]
    gbt = [low(cot[r]) for r in two]
    gb = [g.T for g in gbt]
    grads = {}
    grads["down"] = [[nn(gbt[r], hidden[c]) for r in two] for c in two]
    gh = [nn(gb[0], w_down[0, c]) + nn(gb[1], w_down[1, c]) for c in two]
    g_gate = [low(gh[c] * up[c] * sig[c] * (1.0 + gate[c] * (1.0 - sig[c]))) for c in two]
    g_up = [low(gh[c] * silu[c]) for c in two]
    grads["gate"] = [[nn(n2t[r], g_gate[c]) for r in two] for c in two]
    grads["up"] = [[nn(n2t[r], g_up[c]) for r in two] for c in two]
    g_n2 = [
        nt(w_gate[r, 0], g_gate[0]) + nt(w_gate[r, 1], g_gate[1])
        + nt(w_up[r, 0], g_up[0]) + nt(w_up[r, 1], g_up[1])
        for r in two
    ]
    back, gain_two_grad = norm_back(mid, scale_two, gain_two, g_n2)
    g_mid = [cot[r] + back[r] for r in two]
    gat = [low(g) for g in g_mid]
    ga = [g.T for g in gat]
    grads["out"] = [[nn(ctxt[c], ga[r]) for r in two] for c in two]
    g_ctx = jnp.concatenate(
        [low(nn(w_out[0, c], gat[0]) + nn(w_out[1, c], gat[1])) for c in two], axis=0
    )
    gq, gk, gv = [], [], []
    for h in range(KVH):
        kt, vt, qcat, probs = heads[h]
        gcat = jnp.concatenate([g_ctx[j * 64 : j * 64 + 64] for j in range(3 * h, 3 * h + 3)], axis=1)
        gv.append(low(nt(gcat, low(probs))))
        g_probs = nn(vt.T, gcat)
        g_scores = low(probs * (g_probs - jnp.sum(probs * g_probs, axis=0, keepdims=True)))
        g_q = nn(kt, g_scores) * HD ** (-0.5)
        gq += [low(rotate(g_q[:, j * 128 : j * 128 + 128], cosine, -sine)) for j in range(3)]
        gk.append(low(rotate(nt(qcat, g_scores) * HD ** (-0.5), cosine, -sine)))
    gq, gk, gv = [jnp.concatenate(g, axis=0) for g in (gq, gk, gv)]
    gqt = [gq[:480], gq[480:]]
    gkvt = [jnp.concatenate([gk[c * 160 : c * 160 + 160], gv[c * 160 : c * 160 + 160]], axis=0) for c in two]
    gqkvt = [jnp.concatenate([gqt[c], gkvt[c]], axis=0) for c in two]
    g_n1 = [nn(w_qkv[r, 0], gqkvt[0]) + nn(w_qkv[r, 1], gqkvt[1]) for r in two]
    back, gain_one_grad = norm_back(resid, scale_one, gain_one, g_n1)
    grads["q"] = [[nn(n1t[r], gqt[c].T) for r in two] for c in two]
    grads["kv"] = [
        [
            jnp.concatenate(
                [nn(n1t[r], gkvt[c].T), gain_one_grad[r], gain_two_grad[r], jnp.zeros((480, 62))], axis=1
            )
            for r in two
        ]
        for c in two
    ]
    g_tok = [g_mid[r] + back[r] for r in two]
    return out, g_tok, grads


def on_device(
    tokens, gain_attn, gain_mlp, w_query, w_key, w_value, w_out, w_gate, w_up, w_down, seq_lengths, cotangent
):
    seq = jnp.zeros((8, 128), jnp.int32).at[0:1, 0:3].set(seq_lengths)
    w_qkv = jnp.concatenate([w_query, w_key, w_value], axis=1)
    *full, tok, cot, seq = gather_weights([w_qkv, w_out, w_gate, w_up, w_down], tokens, cotangent, seq)
    gains = [lax.all_gather(g, "row", axis=0).reshape(2, 480, 1) for g in (gain_attn, gain_mlp)]
    out, g_tok, grads = layer(*full, tok, cot, seq, *gains)
    packed = []
    for name, n, _ in STREAMS:
        g = jnp.stack([jnp.stack([low(b) for b in a]) for a in grads[name]])
        packed.append(jnp.pad(g, ((0, 0), (0, 0), (0, ROWS - 480), (0, 0))))
    sums = reduce_grads(packed)
    sums = {s[0]: v[:480] for s, v in zip(STREAMS, sums)}

    def place_rows(parts):
        r = lax.axis_index("row")
        both = jnp.stack(parts)
        mine = lax.dynamic_index_in_dim(both, r, 0, False)
        theirs = lax.ppermute(lax.dynamic_index_in_dim(both, 1 - r, 0, False), "row", [(0, 1), (1, 0)])
        return jnp.where(
            r == 0, jnp.concatenate([mine, theirs], axis=1), jnp.concatenate([theirs, mine], axis=1)
        )

    f32 = {name: v.astype(jnp.float32) for name, v in sums.items()}
    return (
        place_rows(out), place_rows(g_tok), f32["kv"][:, 320], f32["kv"][:, 321],
        f32["q"], f32["kv"][:, :160], f32["kv"][:, 160:320], f32["out"],
        f32["gate"], f32["up"], f32["down"],
    )


def solution(mesh):
    in_specs = (
        P("row", ("tok", "col")), P("row"), P("row"), P("row", "col"), P("row", "col"), P("row", "col"),
        P("col", "row"), P("row", "col"), P("row", "col"), P("row", "col"),
        P(("tok", "row", "col"), None), P("row", ("tok", "col")),
    )
    out_specs = (
        P("row", ("tok", "col")), P("row", ("tok", "col")), P("row"), P("row"), P("row", "col"),
        P("row", "col"), P("row", "col"), P("col", "row"), P("row", "col"), P("row", "col"), P("row", "col"),
    )
    return jax.shard_map(
        on_device, mesh=mesh, in_specs=in_specs, out_specs=out_specs, check_vma=False
    )
```

```python
import math

import jax
import jax.numpy as jnp
from jax import lax
from jax.experimental import pallas as pl
from jax.experimental.pallas import tpu as pltpu
from jax.sharding import PartitionSpec as P

MESH = pl.DeviceIdType.MESH
MIB = 1024 * 1024


def position():
    t = lax.axis_index("tok")
    r = lax.axis_index("row")
    c = lax.axis_index("col")
    return {"x": (t % 2) * 2 + r, "y": (t // 2) % 4, "z": t // 8, "c": c}


def device(place, axis, step):
    p = dict(place)
    p[axis] = (p[axis] + step) % (2 if axis == "c" else 4)
    return (p["z"] * 8 + p["y"] * 2 + p["x"] // 2, p["x"] % 2, p["c"])


def meet(place):
    barrier = pltpu.get_barrier_semaphore()
    partners = [("c", 1)] + [(a, d) for a in "xyz" for d in (1, 2, 3)]
    for axis, step in partners:
        pl.semaphore_signal(
            barrier, inc=1, device_id=device(place, axis, step), device_id_type=MESH
        )
    pl.semaphore_wait(barrier, len(partners))


def send(src, dst, send_sem, recv_sem, target):
    copy = pltpu.make_async_remote_copy(
        src_ref=src, dst_ref=dst, send_sem=send_sem, recv_sem=recv_sem,
        device_id=target, device_id_type=MESH,
    )
    copy.start()
    return copy


ROWS = 512
STREAMS = (
    ("down", 1280, "xyz"),
    ("gate", 1280, "yzx"),
    ("up", 1280, "zxy"),
    ("out", 512, "xyz"),
    ("q", 512, "yzx"),
    ("kv", 384, "zxy"),
)


def aligned(value, unit):
    return pl.multiple_of(value, unit)


class Stream:
    def __init__(self, order, place):
        self.order = order
        self.place = place

    def piece(self, acc, level, owner):
        size, start, lead = ROWS, 0, None
        for depth in range(level + 1):
            axis = self.order[depth]
            index = owner if depth == level else self.place[axis]
            if axis == "x":
                size //= 2
                start = start + (index // 2) * size
                lead = index % 2
            else:
                size //= 4
                start = start + index * size
        rows = pl.ds(aligned(start, 16), size)
        if lead is None:
            return acc.at[:, rows]
        return acc.at[lead, rows]

    def result(self, out, level):
        size, start = ROWS, 0
        for depth in range(level + 1):
            axis = self.order[depth]
            size //= 2 if axis == "x" else 4
            start = start + (self.place[axis] // 2 if axis == "x" else self.place[axis]) * size
        return out.at[pl.ds(aligned(start, 16), size)]

    def shape(self, level, n):
        size, lead = ROWS, 2
        for depth in range(level + 1):
            if self.order[depth] == "x":
                size //= 2
                lead = 1
            else:
                size //= 4
        return (lead, size, n) if lead == 2 else (size, n)


def add_rows(dst, srcs, step=16):
    shape = dst.shape
    if len(shape) == 2:
        views = [(dst, srcs)]
    else:
        views = [(dst.at[k], [s.at[k] for s in srcs]) for k in range(shape[0])]
    rows = shape[-2]
    step = min(step, rows)
    for d, ss in views:
        @pl.loop(0, rows // step)
        def _(i, d=d, ss=ss):
            at = pl.ds(aligned(i * step, step), step)
            total = d[at, :].astype(jnp.float32)
            for s in ss:
                total = total + s[at, :].astype(jnp.float32)
            d[at, :] = total.astype(d.dtype)


D = 960
HQ = 15
KVH = 5
HD = 64
EPS = 1e-05
THETA = 100000.0


def nn(left, right):
    return jnp.dot(left, right, preferred_element_type=jnp.float32)


def nt(left, right):
    return lax.dot_general(
        left, right, (((1,), (1,)), ((), ())), preferred_element_type=jnp.float32
    )


def low(value):
    return value.astype(jnp.bfloat16)


def tables(seq):
    first, second = seq[0:1, 0:1], seq[0:1, 0:1] + seq[0:1, 1:2]

    def segment(index):
        return (index >= first).astype(jnp.int32) + (index >= second).astype(jnp.int32)

    lane = lax.broadcasted_iota(jnp.int32, (1, 128), 1)
    seg_q = segment(lane)
    begin = jnp.where(seg_q == 0, 0, jnp.where(seg_q == 1, first, second))
    place = (lane - begin).astype(jnp.float32)
    ladder = lax.broadcasted_iota(jnp.int32, (32, 128), 0).astype(jnp.float32)
    angle = place * jnp.exp(ladder * (-2.0 * math.log(THETA) / HD))
    rows = lax.broadcasted_iota(jnp.int32, (128, 128), 0)
    lanes = lax.broadcasted_iota(jnp.int32, (128, 128), 1)
    seg_rows = (rows >= first).astype(jnp.int32) + (rows >= second).astype(jnp.int32)
    seg_lanes = (lanes >= first).astype(jnp.int32) + (lanes >= second).astype(jnp.int32)
    allowed = (seg_rows == seg_lanes) & (rows <= lanes)
    return jnp.cos(angle), jnp.sin(angle), allowed


def rotate(head, cosine, sine):
    a, b = head[:32], head[32:]
    return jnp.concatenate([a * cosine - b * sine, b * cosine + a * sine], axis=0)


def features_total(parts):
    return jnp.sum(parts[0], axis=0, keepdims=True) + jnp.sum(parts[1], axis=0, keepdims=True)


def inverse_rms(parts):
    return lax.rsqrt(features_total([p * p for p in parts]) / D + EPS)


def norm_back(resid, scale, gain, grad):
    weighted = [grad[r] * gain[r] for r in range(2)]
    inner = features_total([weighted[r] * resid[r] for r in range(2)]) / D
    grad_resid = [
        weighted[r] * scale - resid[r] * (scale * scale * scale * inner) for r in range(2)
    ]
    grad_gain = [jnp.sum(grad[r] * resid[r] * scale, axis=1, keepdims=True) for r in range(2)]
    return grad_resid, grad_gain

UNIT = 48
BLOCK = 480
QKV = 896
NAMES = [s[0] for s in STREAMS]
N_OF = {s[0]: s[1] for s in STREAMS}


def mega_kernel(*refs):
    k = 5
    src = refs[:k]
    tok, cot, seq, misc = refs[k : k + 4]
    refs = refs[k + 4 :]
    out_ref, g_tok_ref = refs[:2]
    result = dict(zip(NAMES, refs[2:8]))
    refs = refs[8:]
    full, refs = refs[:k], refs[k:]
    w_qkv, w_out, w_gate, w_up, w_down = full
    acc = dict(zip(("down", "gate", "up", "kv"), refs[:4]))
    refs = refs[4:]
    mate, refs = dict(zip(NAMES, refs[:6])), refs[6:]
    got = {name: refs[3 * i : 3 * i + 3] for i, name in enumerate(NAMES)}
    refs = refs[18:]
    (
        seq_in, seq_own, misc_all, tok_all, cot_all, n1t, flat, qkvt, q_rot, k_rot, v_rot, probs_ref,
        ctxt, midt, n2t, gate_ref, up_ref, hidden, gbt, g_gate, g_up, g_midt,
        gat, gan, g_ctx, g_qkvt, out_own, scales,
    ) = refs[:28]
    work = qkvt.at[0:D]
    (
        local_sem, x_send, x_recv, relay_send, relay_recv, wm_send, wm_recv, act_send, act_recv,
        mate_send, mate_recv, rs_send, rs_recv, ag_send, ag_recv, keep_sem, end_send, end_recv,
    ) = refs[28:]
    acc["out"] = w_up.at[:, 0:ROWS, 0:512]
    acc["q"] = w_up.at[:, 0:ROWS, 512:1024]
    stage = {
        "down": acc["gate"].at[:, 0:BLOCK],
        "gate": w_down.at[0],
        "up": w_down.at[1],
        "out": w_gate.at[0, :, 0:512],
        "q": w_gate.at[0, :, 512:1024],
        "kv": w_gate.at[1, :, 0:384],
    }

    place = position()
    r, c = place["x"] % 2, place["c"]
    t = lax.axis_index("tok")
    row_mate, diagonal = (t, 1 - r, c), (t, 1 - r, 1 - c)
    core_mate = device(place, "c", 1)
    barrier = pltpu.get_barrier_semaphore()
    partners = [core_mate] + [device(place, a, d) for a in "xyz" for d in (1, 2, 3)] + [diagonal]
    for target in partners:
        pl.semaphore_signal(barrier, inc=1, device_id=target, device_id_type=MESH)
    pl.semaphore_wait(barrier, len(partners))

    def spot(i, row, col):
        lead, base = (row, col) if i == 1 else (col, row)
        return full[i].at[lead, pl.ds(aligned(base * BLOCK, 16), BLOCK)]

    def part(i, row, col, unit):
        lead, base = (row, col) if i == 1 else (col, row)
        return full[i].at[lead, pl.ds(aligned(base * BLOCK + unit * UNIT, 16), UNIT)]

    late = []
    seq_copy = send(seq, seq_in, act_send.at[2], act_recv.at[2], diagonal)
    misc_copy = send(misc, misc_all.at[r], act_send.at[3], act_recv.at[3], row_mate)
    theirs = pl.ds(aligned((1 - r) * 128, 128), 128)
    mine = pl.ds(aligned(r * 128, 128), 128)
    tok_copy = send(tok.at[:, theirs], tok_all.at[r], act_send.at[0], act_recv.at[0], row_mate)
    locals_ = []

    def local(a, b, sem):
        copy = pltpu.make_async_copy(a, b, sem)
        copy.start()
        return copy

    tok_local = local(tok.at[:, mine], tok_all.at[r], local_sem.at[k])
    cot_local = local(cot.at[:, mine], cot_all.at[r], local_sem.at[k + 1])
    misc_local = local(misc, misc_all.at[r], local_sem.at[k + 2])
    x_in, w_local, w_mate = [], [], []
    for i in range(k):
        arrive = []
        for j, (step, unit) in enumerate(((1, place["y"]), (3, 4 + place["z"]), (1, 8), (3, 9))):
            rows = pl.ds(aligned(unit * UNIT, 16), UNIT)
            arrive.append(
                send(
                    src[i].at[rows], part(i, r, c, unit), x_send.at[i, j], x_recv.at[i, j],
                    device(place, "x", step),
                )
            )
        x_in.append(arrive)
        w_local.append(local(src[i], spot(i, r, c), local_sem.at[i]))
        w_mate.append(send(src[i], spot(i, r, c), wm_send.at[i, 0], wm_recv.at[i, 0], core_mate))
    cot_copy = send(cot.at[:, theirs], cot_all.at[r], act_send.at[1], act_recv.at[1], row_mate)

    relays, forwards = {}, {}

    def relay(i):
        copies = []
        for j, (axis, unit) in enumerate((("y", place["y"]), ("z", 4 + place["z"]))):
            x_in[i][j].wait_recv()
            piece = part(i, 1 - r, c, unit)
            for d in (2, 1, 3):
                copies.append(
                    send(
                        piece, piece, relay_send.at[i, j, d - 1], relay_recv.at[i, j, d - 1],
                        device(place, axis, d),
                    )
                )
        relays[i] = copies

    def forward(i):
        for copy in x_in[i][2:] + relays[i]:
            copy.wait_recv()
        block = spot(i, 1 - r, c)
        forwards[i] = send(block, block, wm_send.at[i, 1], wm_recv.at[i, 1], core_mate)

    def ready(i):
        w_local[i].wait()
        w_mate[i].wait_recv()
        forwards[i].wait_recv()

    def release(i):
        for copy in x_in[i] + relays[i] + [w_mate[i], forwards[i]]:
            copy.wait_send()

    streams = {name: Stream(order, place) for name, _, order in STREAMS}
    mates, flying, level_of, keep = {}, {}, {}, {}

    def to_mate(name):
        i = NAMES.index(name)
        mates[name] = send(stage[name], mate[name], mate_send.at[i], mate_recv.at[i], core_mate)

    def scatter(name, level):
        i, axis = NAMES.index(name), streams[name].order[level]
        flying[name] = [
            send(
                streams[name].piece(acc[name], level, (place[axis] + d) % 4), got[name][level].at[d - 1],
                rs_send.at[i, level, d - 1], rs_recv.at[i, level, d - 1], device(place, axis, d),
            )
            for d in (2, 1, 3)
        ]

    def spread(name, level, source=None):
        i, axis = NAMES.index(name), streams[name].order[level]
        there = streams[name].result(result[name], level)
        flying[name] = [
            send(
                there if source is None else source, there, ag_send.at[i, level, d - 1],
                ag_recv.at[i, level, d - 1], device(place, axis, d),
            )
            for d in ((2,) if axis == "x" else (2, 1, 3))
        ]

    def advance(name):
        step = level_of.get(name, 0)
        level_of[name] = step + 1
        i = NAMES.index(name)
        if step == 0:
            mates[name].wait_recv()
            for lead in range(2):
                theirs = mate[name].at[lead if name == "down" else pl.ds(lead * BLOCK, BLOCK)]
                add_rows(acc[name].at[lead, 0:BLOCK], [theirs])
            scatter(name, 0)
            return
        for copy in flying[name]:
            copy.wait()
        if step <= 3:
            level = step - 1
            own = streams[name].piece(acc[name], level, place[streams[name].order[level]])
            add_rows(own, [got[name][level].at[d] for d in range(3)])
            if level < 2:
                scatter(name, level + 1)
            else:
                keep[name] = local(own, streams[name].result(result[name], 2), keep_sem.at[i])
                spread(name, 2, own)
        elif step <= 5:
            if step == 4:
                keep[name].wait()
            spread(name, 5 - step)

    def wgrad(left, right_of, name, columns=256):
        n = N_OF[name]
        steps = -(-n // columns)

        def block(col, lanes, row):
            return low(nn(left[row * BLOCK : row * BLOCK + BLOCK, :], right_of(col, lanes)))

        def run(col, put):
            if n % columns == 0:
                @pl.loop(0, steps)
                def _(j):
                    lanes = pl.ds(aligned(j * columns, columns), columns)
                    for row in range(2):
                        put(row, lanes, block(col, lanes, row))
            else:
                for row in range(2):
                    put(row, pl.ds(0, n), block(col, pl.ds(0, n), row))

        def put_stage(row, lanes, value):
            if name == "down":
                stage[name][row, :, lanes] = value
            else:
                stage[name][row * BLOCK : row * BLOCK + BLOCK, lanes] = value

        def put_acc(row, lanes, value):
            acc[name][row, 0:BLOCK, lanes] = value

        run(1 - c, put_stage)
        to_mate(name)
        run(c, put_acc)
        for row in range(2):
            acc[name][row, BLOCK:ROWS, :] = jnp.zeros((ROWS - BLOCK, n), jnp.bfloat16)

    two = range(2)
    rows_of = [slice(row * BLOCK, row * BLOCK + BLOCK) for row in two]

    seq_copy.wait()
    seq_own[...] = jnp.where(r == c, seq[...], seq_in[...])
    cosine, sine, allowed = tables(seq_own[...])
    mask = jnp.concatenate([allowed] * 3, axis=1)
    misc_local.wait()
    misc_copy.wait()
    gains = [misc_all[row].T for row in two]
    gain_one = [gains[row][:BLOCK, 0:1] for row in two]
    gain_two = [gains[row][:BLOCK, 1:2] for row in two]
    tok_local.wait()
    tok_copy.wait()
    relay(0)
    relay(1)

    def resid(row):
        return tok_all[row].astype(jnp.float32)

    scales[0:1, :] = inverse_rms([resid(row) for row in two])
    for row in two:
        n1t[rows_of[row], :] = low(resid(row) * scales[0:1, :] * gain_one[row])
    flat[...] = n1t[...].T
    relay(2)
    forward(0)
    relay(3)
    ready(0)
    for col in two:
        both = nn(flat[...], w_qkv[col]).T
        qkvt[col * BLOCK : col * BLOCK + BLOCK, :] = both[:BLOCK]
        qkvt[960 + col * 160 : 1120 + col * 160, :] = both[480:640]
        qkvt[1280 + col * 160 : 1440 + col * 160, :] = both[640:800]
    relay(4)
    forward(1)
    for h in range(KVH):
        k_rot[h * 64 : h * 64 + 64, :] = low(rotate(qkvt[960 + h * 64 : 1024 + h * 64, :], cosine, sine))
        v_rot[h * 64 : h * 64 + 64, :] = low(qkvt[1280 + h * 64 : 1344 + h * 64, :])
        for j in range(3):
            at = (3 * h + j) * 64
            q_rot[h * 64 : h * 64 + 64, j * 128 : j * 128 + 128] = low(rotate(qkvt[at : at + 64, :], cosine, sine))
    for h in range(KVH):
        own = slice(h * 64, h * 64 + 64)
        scores = jnp.where(mask, nn(k_rot[own, :].T, q_rot[own, :]) * HD ** (-0.5), -1e30)
        expo = jnp.exp(scores - jnp.max(scores, axis=0, keepdims=True))
        probs = expo / jnp.sum(expo, axis=0, keepdims=True)
        probs_ref[h] = probs
        context = low(nn(v_rot[own, :], low(probs)))
        for j in range(3):
            at = (3 * h + j) * 64
            ctxt[at : at + 64, :] = context[:, j * 128 : j * 128 + 128]
        if h == 1:
            forward(2)
        if h == 3:
            forward(3)
    flat[...] = ctxt[...].T
    ready(1)
    for row in two:
        midt[rows_of[row], :] = resid(row) + nn(flat[...], w_out[row]).T
    forward(4)
    mids = [midt[rows_of[row], :] for row in two]
    scales[1:2, :] = inverse_rms(mids)
    for row in two:
        n2t[rows_of[row], :] = low(midt[rows_of[row], :] * scales[1:2, :] * gain_two[row])
    flat[...] = n2t[...].T
    ready(2)
    ready(3)

    @pl.loop(0, 10)
    def _(i):
        col = i // 5
        lanes = pl.ds(aligned(i % 5 * 256, 256), 256)
        gate = nn(flat[...], w_gate[col, :, lanes])
        up = nn(flat[...], w_up[col, :, lanes])
        gate_ref[col, :, lanes] = gate
        up_ref[col, :, lanes] = up
        hidden[col, :, lanes] = low(gate * jax.nn.sigmoid(gate) * up)

    cot_local.wait()
    cot_copy.wait()
    for row in two:
        gbt[rows_of[row], :] = low(cot_all[row])
    flat[...] = gbt[...].T
    wgrad(gbt, lambda col, lanes: hidden[col, :, lanes], "down")
    ready(4)

    @pl.loop(0, 10)
    def _(i):
        col = i // 5
        lanes = pl.ds(aligned(i % 5 * 256, 256), 256)
        grad = nn(flat[...], w_down[col, :, lanes])
        gate = gate_ref[col, :, lanes]
        sig = jax.nn.sigmoid(gate)
        g_gate[col, :, lanes] = low(grad * up_ref[col, :, lanes] * sig * (1.0 + gate * (1.0 - sig)))
        g_up[col, :, lanes] = low(grad * (gate * sig))

    advance("down")
    work[...] = midt[...]
    for col in two:
        work[...] += nt(w_down[col], hidden[col])
    out_own[...] = work[...]
    out_copy = send(
        out_own.at[pl.ds(aligned((1 - r) * BLOCK, 16), BLOCK)], out_ref.at[:, mine], end_send.at[0],
        end_recv.at[0], row_mate,
    )
    out_ref[:, mine] = out_own[pl.ds(aligned(r * BLOCK, 16), BLOCK), :]
    release(4)
    mates["down"].wait_send()
    wgrad(n2t, lambda col, lanes: g_gate[col, :, lanes], "gate")
    wgrad(n2t, lambda col, lanes: g_up[col, :, lanes], "up")
    advance("gate")
    work[...] = nt(w_gate[0], g_gate[0]) + nt(w_gate[1], g_gate[1])
    advance("up")
    work[...] += nt(w_up[0], g_up[0]) + nt(w_up[1], g_up[1])
    release(2)
    release(3)
    back, gain_two_grad = norm_back(
        [midt[rows_of[row], :] for row in two], scales[1:2, :], gain_two, [work[rows_of[row], :] for row in two]
    )
    for row in two:
        total = cot_all[row] + back[row]
        g_midt[rows_of[row], :] = total
        gat[rows_of[row], :] = low(total)
    gat[960:992, :] = jnp.zeros((32, 128), jnp.bfloat16)
    for row in two:
        gan[row] = gat[row * BLOCK : row * BLOCK + 512, :].T
    for col in two:
        at = slice(col * BLOCK, col * BLOCK + BLOCK)
        g_ctx[at, :] = low(
            nn(w_out[0, at, :], gat[0:BLOCK, :]) + nn(w_out[1, at, :], gat[BLOCK:960, :])
        )
    def out_block(col, row):
        left = ctxt[pl.ds(aligned(col * BLOCK, 16), BLOCK), :]
        return low(nn(left, gan[row]))

    for row in two:
        stage["out"][row * BLOCK : row * BLOCK + BLOCK, :] = out_block(1 - c, row)
    to_mate("out")
    for row in two:
        acc["out"][row, 0:BLOCK, :] = out_block(c, row)
        acc["out"][row, BLOCK:ROWS, :] = jnp.zeros((ROWS - BLOCK, 512), jnp.bfloat16)
    advance("down")
    for h in range(KVH):
        own = slice(h * 64, h * 64 + 64)
        g_cat = jnp.concatenate(
            [g_ctx[j * 64 : j * 64 + 64, :] for j in range(3 * h, 3 * h + 3)], axis=1
        )
        probs = probs_ref[h]
        g_v = low(nt(g_cat, low(probs)))
        g_probs = nn(v_rot[own, :].T, g_cat)
        g_scores = low(probs * (g_probs - jnp.sum(probs * g_probs, axis=0, keepdims=True)))
        g_q = nn(k_rot[own, :], g_scores) * HD ** (-0.5)
        g_k = low(rotate(nt(q_rot[own, :], g_scores) * HD ** (-0.5), cosine, -sine))
        parts = [(480, 160, h * 64, g_k), (640, 160, h * 64, g_v)]
        for j in range(3):
            g_j = low(rotate(g_q[:, j * 128 : j * 128 + 128], cosine, -sine))
            parts.append((0, 480, (3 * h + j) * 64, g_j))
        for base, width, at, value in parts:
            for half in two:
                row = at + 32 * half
                put = base + row % width
                g_qkvt[row // width, put : put + 32, :] = value[half * 32 : half * 32 + 32]
        if h == 1:
            advance("gate")
        if h == 2:
            advance("up")
    for col in two:
        g_qkvt[col, 800:QKV, :] = jnp.zeros((QKV - 800, 128), jnp.bfloat16)
    advance("out")
    work[0:BLOCK, :] = nn(w_qkv[0, 0:BLOCK, :], g_qkvt[0]) + nn(w_qkv[1, 0:BLOCK, :], g_qkvt[1])
    work[BLOCK:960, :] = nn(w_qkv[0, BLOCK:960, :], g_qkvt[0]) + nn(w_qkv[1, BLOCK:960, :], g_qkvt[1])
    back, gain_one_grad = norm_back(
        [resid(row) for row in two], scales[0:1, :], gain_one, [work[rows_of[row], :] for row in two]
    )
    for row in two:
        g_midt[rows_of[row], :] = g_midt[rows_of[row], :] + back[row]
    lane = lax.broadcasted_iota(jnp.int32, (BLOCK, 384), 1)

    def q_block(col, row):
        return low(nn(n1t[rows_of[row], :], g_qkvt[col, 0:512, :].T))

    def kv_block(col, row):
        value = nn(n1t[rows_of[row], :], g_qkvt[col, 480:864, :].T)
        value = jnp.where(lane == 320, gain_one_grad[row], value)
        return low(jnp.where(lane == 321, gain_two_grad[row], value))

    for name, block, n in (("q", q_block, 512), ("kv", kv_block, 384)):
        for row in two:
            stage[name][row * BLOCK : row * BLOCK + BLOCK, :] = block(1 - c, row)
        to_mate(name)
        for row in two:
            acc[name][row, 0:BLOCK, :] = block(c, row)
            acc[name][row, BLOCK:ROWS, :] = jnp.zeros((ROWS - BLOCK, n), jnp.bfloat16)
    g_copy = send(
        g_midt.at[pl.ds(aligned((1 - r) * BLOCK, 16), BLOCK)], g_tok_ref.at[:, mine], end_send.at[1],
        end_recv.at[1], row_mate,
    )
    g_tok_ref[:, mine] = g_midt[pl.ds(aligned(r * BLOCK, 16), BLOCK), :]
    advance("q")
    advance("kv")
    while any(level_of[name] < 7 for name in NAMES):
        for name in NAMES:
            if level_of[name] < 7:
                advance(name)
    out_copy.wait()
    g_copy.wait()
    for name in NAMES[1:]:
        mates[name].wait_send()
    release(0)
    release(1)


def run_layer(weights, tokens, cotangent, seq, misc):
    bf, f32 = jnp.bfloat16, jnp.float32
    dma = pltpu.SemaphoreType.DMA
    hbm, vmem = pl.BlockSpec(memory_space=pl.ANY), pl.BlockSpec(memory_space=pltpu.VMEM)
    place = {"x": 0, "y": 0, "z": 0, "c": 0}

    def v(shape, dtype=bf):
        return pltpu.VMEM(shape, dtype)

    scratch = [v((2, 2 * BLOCK, w.shape[1])) for w in weights]
    scratch += [v((2, ROWS, N_OF[name])) for name in ("down", "gate", "up", "kv")]
    scratch += [v((2, BLOCK, n) if name == "down" else (2 * BLOCK, n)) for name, n, _ in STREAMS]
    for _, n, order in STREAMS:
        for level in range(3):
            scratch.append(v((3,) + Stream(order, place).shape(level, n)))
    scratch += [
        v((8, 128), jnp.int32), v((8, 128), jnp.int32), v((2, 8, 512), f32), v((2, BLOCK, 128)),
        v((2, BLOCK, 128), f32), v((D, 128)), v((128, D)), v((1600, 128), f32), v((320, 384)),
        v((320, 128)), v((320, 128)), v((KVH, 128, 384), f32), v((D, 128)), v((D, 128), f32),
        v((D, 128)), v((2, 128, 1280), f32), v((2, 128, 1280), f32), v((2, 128, 1280)),
        v((D, 128)), v((2, 128, 1280)), v((2, 128, 1280)),
        v((D, 128), f32), v((992, 128)), v((2, 128, 512)), v((D, 128)), v((2, QKV, 128)), v((D, 128), f32),
        v((8, 128), f32),
    ]
    scratch += [
        dma((8,)), dma((5, 4)), dma((5, 4)), dma((5, 2, 3)), dma((5, 2, 3)), dma((5, 2)), dma((5, 2)),
        dma((4,)), dma((4,)), dma((6,)), dma((6,)), dma((6, 3, 3)), dma((6, 3, 3)), dma((6, 3, 3)),
        dma((6, 3, 3)), dma((6,)), dma((2,)), dma((2,)),
    ]
    return pl.pallas_call(
        mega_kernel,
        out_shape=[jax.ShapeDtypeStruct((BLOCK, 256), f32)] * 2
        + [jax.ShapeDtypeStruct((ROWS, n), bf) for _, n, _ in STREAMS],
        in_specs=[hbm] * 7 + [vmem] * 2,
        out_specs=[vmem] * 2 + [hbm] * 6,
        scratch_shapes=scratch,
        compiler_params=pltpu.CompilerParams(
            collective_id=1, has_side_effects=True, vmem_limit_bytes=63 * MIB
        ),
        cost_estimate=pl.CostEstimate(flops=8 * 10**9, bytes_accessed=60 * MIB, transcendentals=0),
    )(*weights, tokens, cotangent, seq, misc)


def on_device(
    tokens, gain_attn, gain_mlp, w_query, w_key, w_value, w_out, w_gate, w_up, w_down, seq_lengths, cotangent
):
    seq = jnp.pad(seq_lengths, ((0, 7), (0, 125)))
    misc = jnp.pad(jnp.stack([gain_attn, gain_mlp]), ((0, 6), (0, 32)))
    blank = jnp.zeros((BLOCK, QKV - 800), jnp.bfloat16)
    w_qkv = jnp.concatenate([w_query, w_key, w_value, blank], axis=1)
    out, g_tok, *sums = run_layer([w_qkv, w_out, w_gate, w_up, w_down], tokens, cotangent, seq, misc)
    f32 = {name: v[:BLOCK].astype(jnp.float32) for name, v in zip(NAMES, sums)}
    return (
        out, g_tok, f32["kv"][:, 320], f32["kv"][:, 321],
        f32["q"][:, :480], f32["kv"][:, :160], f32["kv"][:, 160:320], f32["out"][:, :480],
        f32["gate"], f32["up"], f32["down"],
    )

def solution(mesh):
    in_specs = (
        P("row", ("tok", "col")), P("row"), P("row"), P("row", "col"), P("row", "col"), P("row", "col"),
        P("col", "row"), P("row", "col"), P("row", "col"), P("row", "col"),
        P(("tok", "row", "col"), None), P("row", ("tok", "col")),
    )
    out_specs = (
        P("row", ("tok", "col")), P("row", ("tok", "col")), P("row"), P("row"), P("row", "col"),
        P("row", "col"), P("row", "col"), P("col", "row"), P("row", "col"), P("row", "col"), P("row", "col"),
    )
    return jax.shard_map(
        on_device, mesh=mesh, in_specs=in_specs, out_specs=out_specs, check_vma=False
    )
```

```python
import math

import jax
import jax.numpy as jnp
from jax import lax
from jax.experimental import pallas as pl
from jax.experimental.pallas import tpu as pltpu
from jax.sharding import PartitionSpec as P

MESH = pl.DeviceIdType.MESH
MIB = 1024 * 1024


def position():
    t = lax.axis_index("tok")
    r = lax.axis_index("row")
    c = lax.axis_index("col")
    return {"x": (t % 2) * 2 + r, "y": (t // 2) % 4, "z": t // 8, "c": c}


def device(place, axis, step):
    p = dict(place)
    p[axis] = (p[axis] + step) % (2 if axis == "c" else 4)
    return (p["z"] * 8 + p["y"] * 2 + p["x"] // 2, p["x"] % 2, p["c"])


def meet(place):
    barrier = pltpu.get_barrier_semaphore()
    partners = [("c", 1)] + [(a, d) for a in "xyz" for d in (1, 2, 3)]
    for axis, step in partners:
        pl.semaphore_signal(
            barrier, inc=1, device_id=device(place, axis, step), device_id_type=MESH
        )
    pl.semaphore_wait(barrier, len(partners))


def send(src, dst, send_sem, recv_sem, target):
    copy = pltpu.make_async_remote_copy(
        src_ref=src, dst_ref=dst, send_sem=send_sem, recv_sem=recv_sem,
        device_id=target, device_id_type=MESH,
    )
    copy.start()
    return copy


ROWS = 512
STREAMS = (
    ("down", 1280, "xyz"),
    ("gate", 1280, "yzx"),
    ("up", 1280, "zxy"),
    ("out", 512, "xyz"),
    ("q", 512, "yzx"),
    ("kv", 384, "zxy"),
)


def aligned(value, unit):
    return pl.multiple_of(value, unit)


class Stream:
    def __init__(self, order, place):
        self.order = order
        self.place = place

    def piece(self, acc, level, owner):
        size, start, lead = ROWS, 0, None
        for depth in range(level + 1):
            axis = self.order[depth]
            index = owner if depth == level else self.place[axis]
            if axis == "x":
                size //= 2
                start = start + (index // 2) * size
                lead = index % 2
            else:
                size //= 4
                start = start + index * size
        rows = pl.ds(aligned(start, 16), size)
        if lead is None:
            return acc.at[:, rows]
        return acc.at[lead, rows]

    def result(self, out, level):
        size, start = ROWS, 0
        for depth in range(level + 1):
            axis = self.order[depth]
            size //= 2 if axis == "x" else 4
            start = start + (self.place[axis] // 2 if axis == "x" else self.place[axis]) * size
        return out.at[pl.ds(aligned(start, 16), size)]

    def shape(self, level, n):
        size, lead = ROWS, 2
        for depth in range(level + 1):
            if self.order[depth] == "x":
                size //= 2
                lead = 1
            else:
                size //= 4
        return (lead, size, n) if lead == 2 else (size, n)


def add_rows(dst, srcs, step=16):
    shape = dst.shape
    if len(shape) == 2:
        views = [(dst, srcs)]
    else:
        views = [(dst.at[k], [s.at[k] for s in srcs]) for k in range(shape[0])]
    rows = shape[-2]
    step = min(step, rows)
    for d, ss in views:
        @pl.loop(0, rows // step)
        def _(i, d=d, ss=ss):
            at = pl.ds(aligned(i * step, step), step)
            total = d[at, :].astype(jnp.float32)
            for s in ss:
                total = total + s[at, :].astype(jnp.float32)
            d[at, :] = total.astype(d.dtype)


D = 960
HQ = 15
KVH = 5
HD = 64
EPS = 1e-05
THETA = 100000.0


def nn(left, right):
    return jnp.dot(left, right, preferred_element_type=jnp.float32)


def nt(left, right):
    return lax.dot_general(
        left, right, (((1,), (1,)), ((), ())), preferred_element_type=jnp.float32
    )


def low(value):
    return value.astype(jnp.bfloat16)


def tables(seq):
    first, second = seq[0:1, 0:1], seq[0:1, 0:1] + seq[0:1, 1:2]

    def segment(index):
        return (index >= first).astype(jnp.int32) + (index >= second).astype(jnp.int32)

    lane = lax.broadcasted_iota(jnp.int32, (1, 128), 1)
    seg_q = segment(lane)
    begin = jnp.where(seg_q == 0, 0, jnp.where(seg_q == 1, first, second))
    place = (lane - begin).astype(jnp.float32)
    ladder = lax.broadcasted_iota(jnp.int32, (32, 128), 0).astype(jnp.float32)
    angle = place * jnp.exp(ladder * (-2.0 * math.log(THETA) / HD))
    rows = lax.broadcasted_iota(jnp.int32, (128, 128), 0)
    lanes = lax.broadcasted_iota(jnp.int32, (128, 128), 1)
    seg_rows = (rows >= first).astype(jnp.int32) + (rows >= second).astype(jnp.int32)
    seg_lanes = (lanes >= first).astype(jnp.int32) + (lanes >= second).astype(jnp.int32)
    allowed = (seg_rows == seg_lanes) & (rows <= lanes)
    return jnp.cos(angle), jnp.sin(angle), allowed


def rotate(head, cosine, sine):
    a, b = head[:32], head[32:]
    return jnp.concatenate([a * cosine - b * sine, b * cosine + a * sine], axis=0)


def features_total(parts):
    return jnp.sum(parts[0], axis=0, keepdims=True) + jnp.sum(parts[1], axis=0, keepdims=True)


def inverse_rms(parts):
    return lax.rsqrt(features_total([p * p for p in parts]) / D + EPS)


def norm_back(resid, scale, gain, grad):
    weighted = [grad[r] * gain[r] for r in range(2)]
    inner = features_total([weighted[r] * resid[r] for r in range(2)]) / D
    grad_resid = [
        weighted[r] * scale - resid[r] * (scale * scale * scale * inner) for r in range(2)
    ]
    grad_gain = [jnp.sum(grad[r] * resid[r] * scale, axis=1, keepdims=True) for r in range(2)]
    return grad_resid, grad_gain

BLOCK = 480
QKV = 896
NAMES = [s[0] for s in STREAMS]
N_OF = {s[0]: s[1] for s in STREAMS}


def mega_kernel(*refs):
    k = 5
    src = refs[:k]
    tok, cot, seq, misc = refs[k : k + 4]
    refs = refs[k + 4 :]
    out_ref, g_tok_ref = refs[:2]
    result = dict(zip(NAMES, refs[2:8]))
    refs = refs[8:]
    full, refs = refs[:k], refs[k:]
    w_qkv, w_out, w_gate, w_up, w_down = full
    acc = dict(zip(("down", "gate", "up", "kv"), refs[:4]))
    refs = refs[4:]
    mate, refs = dict(zip(NAMES, refs[:6])), refs[6:]
    got = {name: refs[3 * i : 3 * i + 3] for i, name in enumerate(NAMES)}
    refs = refs[18:]
    (
        seq_in, seq_own, misc_all, tok_all, cot_all, n1t, flat, qkvt, q_rot, k_rot, v_rot, probs_ref,
        ctxt, midt, n2t, gate_ref, up_ref, hidden, gbt, g_gate, g_up, g_midt,
        gat, gan, g_ctx, g_qkvt, out_own, scales, cot_out, cot_low, cot_got,
    ) = refs[:31]
    work = qkvt.at[0:D]
    (
        local_sem, x_send, x_recv, relay_send, relay_recv, wm_send, wm_recv, act_send, act_recv,
        mate_send, mate_recv, rs_recv, ag_recv, keep_sem, end_send, end_recv, out_sem, ring_recv, last_recv,
    ) = refs[31:]
    acc["out"] = w_up.at[:, 0:ROWS, 0:512]
    acc["q"] = w_up.at[:, 0:ROWS, 512:1024]
    stage = {
        "down": acc["gate"].at[:, 0:BLOCK],
        "gate": w_down.at[0],
        "up": w_down.at[1],
        "out": w_gate.at[0, :, 0:512],
        "q": w_gate.at[0, :, 512:1024],
        "kv": w_gate.at[1, :, 0:384],
    }

    place = position()
    r, c = place["x"] % 2, place["c"]
    t = lax.axis_index("tok")
    row_mate, diagonal = (t, 1 - r, c), (t, 1 - r, 1 - c)
    core_mate = device(place, "c", 1)
    barrier = pltpu.get_barrier_semaphore()
    partners = [core_mate] + [device(place, a, d) for a in "xyz" for d in (1, 2, 3)] + [diagonal]
    for target in partners:
        pl.semaphore_signal(barrier, inc=1, device_id=target, device_id_type=MESH)
    pl.semaphore_wait(barrier, len(partners))

    def spot(i, row, col):
        lead, base = (row, col) if i == 1 else (col, row)
        return full[i].at[lead, pl.ds(aligned(base * BLOCK, 16), BLOCK)]

    def part(i, row, col, start, count):
        lead, base = (row, col) if i == 1 else (col, row)
        return full[i].at[lead, pl.ds(aligned(base * BLOCK + start, 16), count)]

    near, far = 1 + 2 * r, 3 - 2 * r
    x_parts = (
        (far, place["y"] * 64, 64), (near, 256 + place["z"] * 48, 48), (far, 448, 16), (near, 464, 16)
    )

    late = []
    seq_copy = send(seq, seq_in, act_send.at[2], act_recv.at[2], diagonal)
    misc_copy = send(misc, misc_all.at[r], act_send.at[3], act_recv.at[3], row_mate)
    theirs = pl.ds(aligned((1 - r) * 128, 128), 128)
    mine = pl.ds(aligned(r * 128, 128), 128)
    tok_copy = send(tok.at[:, theirs], tok_all.at[r], act_send.at[0], act_recv.at[0], row_mate)
    locals_ = []

    def local(a, b, sem):
        copy = pltpu.make_async_copy(a, b, sem)
        copy.start()
        return copy

    tok_local = local(tok.at[:, mine], tok_all.at[r], local_sem.at[k])
    cot_local = local(cot.at[:, mine], cot_all.at[r], local_sem.at[k + 1])
    cot_theirs = local(cot.at[:, theirs], cot_out, local_sem.at[k + 3])
    misc_local = local(misc, misc_all.at[r], local_sem.at[k + 2])
    x_in, w_local, w_mate = [], [], []

    def to_x(i, j):
        step, start, count = x_parts[j]
        return send(
            src[i].at[pl.ds(aligned(start, 16), count)], part(i, r, c, start, count), x_send.at[i, j],
            x_recv.at[i, j], device(place, "x", step),
        )

    for i in range(k):
        arrive = []
        for j in range(2):
            arrive.append(to_x(i, j))
        x_in.append(arrive)
        w_local.append(local(src[i], spot(i, r, c), local_sem.at[i]))
        w_mate.append(send(src[i], spot(i, r, c), wm_send.at[i, 0], wm_recv.at[i, 0], core_mate))

    relays, forwards = {}, {}

    def pass_on(i, axis, start, count, d, slot):
        piece = part(i, 1 - r, c, start, count)
        return send(
            piece, piece, relay_send.at[i, slot], relay_recv.at[i, slot], device(place, axis, d)
        )

    def relay(i):
        x_in[i][0].wait_recv()
        relays[i] = [pass_on(i, "y", place["y"] * 64, 64, d, slot) for slot, d in ((0, 1), (1, 3))]
        x_in[i][1].wait_recv()
        relays[i] += [
            pass_on(i, "z", 256 + place["z"] * 48, 48, d, slot) for slot, d in ((2, 2), (3, 1), (4, 3))
        ]
        x_in[i] += [to_x(i, 2), to_x(i, 3)]

    def relay_on(i):
        relays[i][0].wait_recv()
        relays[i].append(pass_on(i, "y", (place["y"] + 3) % 4 * 64, 32, 1, 5))
        relays[i][1].wait_recv()
        relays[i].append(pass_on(i, "y", (place["y"] + 1) % 4 * 64 + 32, 32, 3, 6))

    def forward(i):
        for copy in x_in[i][2:] + relays[i][2:]:
            copy.wait_recv()
        block = spot(i, 1 - r, c)
        forwards[i] = send(block, block, wm_send.at[i, 1], wm_recv.at[i, 1], core_mate)

    def ready(i):
        w_local[i].wait()
        w_mate[i].wait_recv()
        forwards[i].wait_recv()

    def release(i):
        for copy in x_in[i] + relays[i] + [w_mate[i], forwards[i]]:
            copy.wait_send()

    streams = {name: Stream(order, place) for name, _, order in STREAMS}
    mates, flying, level_of, keep = {}, {}, {}, {}

    def to_mate(name):
        i = NAMES.index(name)
        mates[name] = send(stage[name], mate[name], mate_send.at[i], mate_recv.at[i], core_mate)

    def scatter(name, level):
        i, axis = NAMES.index(name), streams[name].order[level]
        flying[name] = [
            send(
                streams[name].piece(acc[name], level, (place[axis] + d) % 4), got[name][level].at[d - 1],
                out_sem.at[i, d - 1], rs_recv.at[i, level - 1, d - 1], device(place, axis, d),
            )
            for d in (2, 1, 3)
        ]

    def spread(name, level, source=None):
        i, axis = NAMES.index(name), streams[name].order[level]
        there = streams[name].result(result[name], level)
        flying[name] = [
            send(
                there if source is None else source, there, out_sem.at[i, d - 1],
                ag_recv.at[i, level - 1, d - 1] if level else last_recv.at[i, 0, 0], device(place, axis, d),
            )
            for d in ((2,) if axis == "x" else (2, 1, 3))
        ]

    def half_of(name, owner, side):
        if streams[name].order[0] == "x":
            return acc[name].at[owner % 2, pl.ds(aligned(owner // 2 * 256 + side * 128, 16), 128)]
        return acc[name].at[side, pl.ds(aligned(owner * 128, 16), 128)]

    def ring(name, slot, source, step):
        i, axis = NAMES.index(name), streams[name].order[0]
        return send(
            source, got[name][0].at[slot], out_sem.at[i, slot], ring_recv.at[i, slot], device(place, axis, step)
        )

    def advance(name):
        step = level_of.get(name, 0)
        level_of[name] = step + 1
        i = NAMES.index(name)
        axis = streams[name].order[0]
        me = place[axis]
        after, across, before = [(me + d) % 4 for d in (1, 2, 3)]
        if step == 0:
            mates[name].wait_recv()
            for lead in range(2):
                theirs = mate[name].at[lead if name == "down" else pl.ds(lead * BLOCK, BLOCK)]
                add_rows(acc[name].at[lead, 0:BLOCK], [theirs])
            flying[name] = [
                ring(name, 0, half_of(name, across, 0), 1),
                ring(name, 1, half_of(name, across, 1), 3),
                ring(name, 2, half_of(name, after, 1), 1),
                ring(name, 3, half_of(name, before, 0), 3),
            ]
            return
        if step == 1:
            for copy, owner, side in ((flying[name][0], after, 0), (flying[name][1], before, 1)):
                copy.wait_recv()
                add_rows(half_of(name, owner, side), [got[name][0].at[side]])
            flying[name] += [
                ring(name, 4, half_of(name, after, 0), 1),
                ring(name, 5, half_of(name, before, 1), 3),
            ]
            return
        if step == 2:
            for copy in flying[name][:2]:
                copy.wait_send()
            for copy in flying[name][2:]:
                copy.wait()
            add_rows(half_of(name, me, 0), [got[name][0].at[3], got[name][0].at[4]])
            add_rows(half_of(name, me, 1), [got[name][0].at[2], got[name][0].at[5]])
            scatter(name, 1)
            return
        for copy in flying[name]:
            copy.wait()
        if step <= 4:
            level = step - 2
            own = streams[name].piece(acc[name], level, place[streams[name].order[level]])
            add_rows(own, [got[name][level].at[d] for d in range(3)])
            if level < 2:
                scatter(name, level + 1)
            else:
                keep[name] = local(own, streams[name].result(result[name], 2), keep_sem.at[i])
                spread(name, 2, own)
        elif step == 5:
            keep[name].wait()
            spread(name, 1)
        elif step == 6 and axis == "x":
            spread(name, 0)
        elif step in (6, 7) and axis != "x":
            base = [aligned(p * 128, 16) for p in (me, before, after)]
            if step == 6:
                pieces = [pl.ds(base[0], 128)] * 2
            else:
                pieces = [pl.ds(base[1], 64), pl.ds(base[2] + 64, 64)]
            flying[name] = [
                send(
                    result[name].at[rows], result[name].at[rows], out_sem.at[i, d // 2],
                    last_recv.at[i, step - 6, d // 2], device(place, axis, d),
                )
                for rows, d in zip(pieces, (1, 3))
            ]
        else:
            flying[name] = []

    def wgrad(left, right_of, name, columns=256):
        n = N_OF[name]
        steps = -(-n // columns)

        def block(col, lanes, row):
            return low(nn(left[row * BLOCK : row * BLOCK + BLOCK, :], right_of(col, lanes)))

        def run(col, put):
            if n % columns == 0:
                @pl.loop(0, steps)
                def _(j):
                    lanes = pl.ds(aligned(j * columns, columns), columns)
                    for row in range(2):
                        put(row, lanes, block(col, lanes, row))
            else:
                for row in range(2):
                    put(row, pl.ds(0, n), block(col, pl.ds(0, n), row))

        def put_stage(row, lanes, value):
            if name == "down":
                stage[name][row, :, lanes] = value
            else:
                stage[name][row * BLOCK : row * BLOCK + BLOCK, lanes] = value

        def put_acc(row, lanes, value):
            acc[name][row, 0:BLOCK, lanes] = value

        run(1 - c, put_stage)
        to_mate(name)
        run(c, put_acc)
        for row in range(2):
            acc[name][row, BLOCK:ROWS, :] = jnp.zeros((ROWS - BLOCK, n), jnp.bfloat16)

    two = range(2)
    rows_of = [slice(row * BLOCK, row * BLOCK + BLOCK) for row in two]

    seq_copy.wait()
    seq_own[...] = jnp.where(r == c, seq[...], seq_in[...])
    cosine, sine, allowed = tables(seq_own[...])
    mask = jnp.concatenate([allowed] * 3, axis=1)
    misc_local.wait()
    misc_copy.wait()
    gains = [misc_all[row].T for row in two]
    gain_one = [gains[row][:BLOCK, 0:1] for row in two]
    gain_two = [gains[row][:BLOCK, 1:2] for row in two]
    tok_local.wait()
    tok_copy.wait()
    relay(0)
    relay(1)

    def resid(row):
        return tok_all[row].astype(jnp.float32)

    scales[0:1, :] = inverse_rms([resid(row) for row in two])
    for row in two:
        n1t[rows_of[row], :] = low(resid(row) * scales[0:1, :] * gain_one[row])
    flat[...] = n1t[...].T
    relay_on(0)
    relay(2)
    relay_on(1)
    relay(3)
    forward(0)
    relay(4)
    relay_on(2)
    cot_theirs.wait()
    cot_low[...] = low(cot_out[...])
    cot_copy = send(cot_low, cot_got, act_send.at[1], act_recv.at[1], row_mate)
    ready(0)
    for col in two:
        both = nn(flat[...], w_qkv[col]).T
        qkvt[col * BLOCK : col * BLOCK + BLOCK, :] = both[:BLOCK]
        qkvt[960 + col * 160 : 1120 + col * 160, :] = both[480:640]
        qkvt[1280 + col * 160 : 1440 + col * 160, :] = both[640:800]
    forward(1)
    relay_on(3)
    relay_on(4)
    for h in range(KVH):
        k_rot[h * 64 : h * 64 + 64, :] = low(rotate(qkvt[960 + h * 64 : 1024 + h * 64, :], cosine, sine))
        v_rot[h * 64 : h * 64 + 64, :] = low(qkvt[1280 + h * 64 : 1344 + h * 64, :])
        for j in range(3):
            at = (3 * h + j) * 64
            q_rot[h * 64 : h * 64 + 64, j * 128 : j * 128 + 128] = low(rotate(qkvt[at : at + 64, :], cosine, sine))
    for h in range(KVH):
        own = slice(h * 64, h * 64 + 64)
        scores = jnp.where(mask, nn(k_rot[own, :].T, q_rot[own, :]) * HD ** (-0.5), -1e30)
        expo = jnp.exp(scores - jnp.max(scores, axis=0, keepdims=True))
        probs = expo / jnp.sum(expo, axis=0, keepdims=True)
        probs_ref[h] = probs
        context = low(nn(v_rot[own, :], low(probs)))
        for j in range(3):
            at = (3 * h + j) * 64
            ctxt[at : at + 64, :] = context[:, j * 128 : j * 128 + 128]
        if h == 1:
            forward(2)
        if h == 3:
            forward(3)
    flat[...] = ctxt[...].T
    ready(1)
    for row in two:
        midt[rows_of[row], :] = resid(row) + nn(flat[...], w_out[row]).T
    forward(4)
    mids = [midt[rows_of[row], :] for row in two]
    scales[1:2, :] = inverse_rms(mids)
    for row in two:
        n2t[rows_of[row], :] = low(midt[rows_of[row], :] * scales[1:2, :] * gain_two[row])
    flat[...] = n2t[...].T
    ready(2)
    ready(3)

    @pl.loop(0, 10)
    def _(i):
        col = i // 5
        lanes = pl.ds(aligned(i % 5 * 256, 256), 256)
        gate = nn(flat[...], w_gate[col, :, lanes])
        up = nn(flat[...], w_up[col, :, lanes])
        gate_ref[col, :, lanes] = gate
        up_ref[col, :, lanes] = up
        hidden[col, :, lanes] = low(gate * jax.nn.sigmoid(gate) * up)

    cot_local.wait()
    cot_copy.wait()
    cot_all[1 - r] = cot_got[...].astype(jnp.float32)
    for row in two:
        gbt[rows_of[row], :] = low(cot_all[row])
    flat[...] = gbt[...].T
    wgrad(gbt, lambda col, lanes: hidden[col, :, lanes], "down")
    ready(4)

    @pl.loop(0, 10)
    def _(i):
        col = i // 5
        lanes = pl.ds(aligned(i % 5 * 256, 256), 256)
        grad = nn(flat[...], w_down[col, :, lanes])
        gate = gate_ref[col, :, lanes]
        sig = jax.nn.sigmoid(gate)
        g_gate[col, :, lanes] = low(grad * up_ref[col, :, lanes] * sig * (1.0 + gate * (1.0 - sig)))
        g_up[col, :, lanes] = low(grad * (gate * sig))

    advance("down")
    work[...] = midt[...]
    for col in two:
        work[...] += nt(w_down[col], hidden[col])
    out_own[...] = work[...]
    out_copy = send(
        out_own.at[pl.ds(aligned((1 - r) * BLOCK, 16), BLOCK)], out_ref.at[:, mine], end_send.at[0],
        end_recv.at[0], row_mate,
    )
    out_ref[:, mine] = out_own[pl.ds(aligned(r * BLOCK, 16), BLOCK), :]
    release(4)
    mates["down"].wait_send()
    wgrad(n2t, lambda col, lanes: g_gate[col, :, lanes], "gate")
    wgrad(n2t, lambda col, lanes: g_up[col, :, lanes], "up")
    advance("gate")
    work[...] = nt(w_gate[0], g_gate[0]) + nt(w_gate[1], g_gate[1])
    advance("up")
    work[...] += nt(w_up[0], g_up[0]) + nt(w_up[1], g_up[1])
    release(2)
    release(3)
    back, gain_two_grad = norm_back(
        [midt[rows_of[row], :] for row in two], scales[1:2, :], gain_two, [work[rows_of[row], :] for row in two]
    )
    for row in two:
        total = cot_all[row] + back[row]
        g_midt[rows_of[row], :] = total
        gat[rows_of[row], :] = low(total)
    gat[960:992, :] = jnp.zeros((32, 128), jnp.bfloat16)
    for row in two:
        gan[row] = gat[row * BLOCK : row * BLOCK + 512, :].T
    for col in two:
        at = slice(col * BLOCK, col * BLOCK + BLOCK)
        g_ctx[at, :] = low(
            nn(w_out[0, at, :], gat[0:BLOCK, :]) + nn(w_out[1, at, :], gat[BLOCK:960, :])
        )
    def out_block(col, row):
        left = ctxt[pl.ds(aligned(col * BLOCK, 16), BLOCK), :]
        return low(nn(left, gan[row]))

    for row in two:
        stage["out"][row * BLOCK : row * BLOCK + BLOCK, :] = out_block(1 - c, row)
    to_mate("out")
    for row in two:
        acc["out"][row, 0:BLOCK, :] = out_block(c, row)
        acc["out"][row, BLOCK:ROWS, :] = jnp.zeros((ROWS - BLOCK, 512), jnp.bfloat16)
    advance("down")
    for h in range(KVH):
        own = slice(h * 64, h * 64 + 64)
        g_cat = jnp.concatenate(
            [g_ctx[j * 64 : j * 64 + 64, :] for j in range(3 * h, 3 * h + 3)], axis=1
        )
        probs = probs_ref[h]
        g_v = low(nt(g_cat, low(probs)))
        g_probs = nn(v_rot[own, :].T, g_cat)
        g_scores = low(probs * (g_probs - jnp.sum(probs * g_probs, axis=0, keepdims=True)))
        g_q = nn(k_rot[own, :], g_scores) * HD ** (-0.5)
        g_k = low(rotate(nt(q_rot[own, :], g_scores) * HD ** (-0.5), cosine, -sine))
        parts = [(480, 160, h * 64, g_k), (640, 160, h * 64, g_v)]
        for j in range(3):
            g_j = low(rotate(g_q[:, j * 128 : j * 128 + 128], cosine, -sine))
            parts.append((0, 480, (3 * h + j) * 64, g_j))
        for base, width, at, value in parts:
            for half in two:
                row = at + 32 * half
                put = base + row % width
                g_qkvt[row // width, put : put + 32, :] = value[half * 32 : half * 32 + 32]
        if h == 1:
            advance("gate")
        if h == 2:
            advance("up")
    for col in two:
        g_qkvt[col, 800:QKV, :] = jnp.zeros((QKV - 800, 128), jnp.bfloat16)
    advance("out")
    work[0:BLOCK, :] = nn(w_qkv[0, 0:BLOCK, :], g_qkvt[0]) + nn(w_qkv[1, 0:BLOCK, :], g_qkvt[1])
    work[BLOCK:960, :] = nn(w_qkv[0, BLOCK:960, :], g_qkvt[0]) + nn(w_qkv[1, BLOCK:960, :], g_qkvt[1])
    back, gain_one_grad = norm_back(
        [resid(row) for row in two], scales[0:1, :], gain_one, [work[rows_of[row], :] for row in two]
    )
    for row in two:
        g_midt[rows_of[row], :] = g_midt[rows_of[row], :] + back[row]
    lane = lax.broadcasted_iota(jnp.int32, (BLOCK, 384), 1)

    def q_block(col, row):
        return low(nn(n1t[rows_of[row], :], g_qkvt[col, 0:512, :].T))

    def kv_block(col, row):
        value = nn(n1t[rows_of[row], :], g_qkvt[col, 480:864, :].T)
        value = jnp.where(lane == 320, gain_one_grad[row], value)
        return low(jnp.where(lane == 321, gain_two_grad[row], value))

    for name, block, n in (("q", q_block, 512), ("kv", kv_block, 384)):
        for row in two:
            stage[name][row * BLOCK : row * BLOCK + BLOCK, :] = block(1 - c, row)
        to_mate(name)
        for row in two:
            acc[name][row, 0:BLOCK, :] = block(c, row)
            acc[name][row, BLOCK:ROWS, :] = jnp.zeros((ROWS - BLOCK, n), jnp.bfloat16)
    g_copy = send(
        g_midt.at[pl.ds(aligned((1 - r) * BLOCK, 16), BLOCK)], g_tok_ref.at[:, mine], end_send.at[1],
        end_recv.at[1], row_mate,
    )
    g_tok_ref[:, mine] = g_midt[pl.ds(aligned(r * BLOCK, 16), BLOCK), :]
    advance("q")
    advance("kv")
    while any(level_of[name] < 9 for name in NAMES):
        for name in NAMES:
            if level_of[name] < 9:
                advance(name)
    out_copy.wait()
    g_copy.wait()
    for name in NAMES[1:]:
        mates[name].wait_send()
    release(0)
    release(1)


def run_layer(weights, tokens, cotangent, seq, misc):
    bf, f32 = jnp.bfloat16, jnp.float32
    dma = pltpu.SemaphoreType.DMA
    hbm, vmem = pl.BlockSpec(memory_space=pl.ANY), pl.BlockSpec(memory_space=pltpu.VMEM)
    place = {"x": 0, "y": 0, "z": 0, "c": 0}

    def v(shape, dtype=bf):
        return pltpu.VMEM(shape, dtype)

    scratch = [v((2, 2 * BLOCK, w.shape[1])) for w in weights]
    scratch += [v((2, ROWS, N_OF[name])) for name in ("down", "gate", "up", "kv")]
    scratch += [v((2, BLOCK, n) if name == "down" else (2 * BLOCK, n)) for name, n, _ in STREAMS]
    for _, n, order in STREAMS:
        for level in range(3):
            scratch.append(v((3,) + Stream(order, place).shape(level, n) if level else (6, 128, n)))
    scratch += [
        v((8, 128), jnp.int32), v((8, 128), jnp.int32), v((2, 8, 512), f32), v((2, BLOCK, 128)),
        v((2, BLOCK, 128), f32), v((D, 128)), v((128, D)), v((1600, 128), f32), v((320, 384)),
        v((320, 128)), v((320, 128)), v((KVH, 128, 384), f32), v((D, 128)), v((D, 128), f32),
        v((D, 128)), v((2, 128, 1280), f32), v((2, 128, 1280), f32), v((2, 128, 1280)),
        v((D, 128)), v((2, 128, 1280)), v((2, 128, 1280)),
        v((D, 128), f32), v((992, 128)), v((2, 128, 512)), v((D, 128)), v((2, QKV, 128)), v((D, 128), f32),
        v((8, 128), f32), v((BLOCK, 128), f32), v((BLOCK, 128)), v((BLOCK, 128)),
    ]
    scratch += [
        dma((9,)), dma((5, 4)), dma((5, 4)), dma((5, 7)), dma((5, 7)), dma((5, 2)), dma((5, 2)),
        dma((4,)), dma((4,)), dma((6,)), dma((6,)), dma((6, 2, 3)), dma((6, 2, 3)),
        dma((6,)), dma((2,)), dma((2,)), dma((6, 6)), dma((6, 6)), dma((6, 2, 2)),
    ]
    return pl.pallas_call(
        mega_kernel,
        out_shape=[jax.ShapeDtypeStruct((BLOCK, 256), f32)] * 2
        + [jax.ShapeDtypeStruct((ROWS, n), bf) for _, n, _ in STREAMS],
        in_specs=[hbm] * 7 + [vmem] * 2,
        out_specs=[vmem] * 2 + [hbm] * 6,
        scratch_shapes=scratch,
        compiler_params=pltpu.CompilerParams(
            collective_id=1, has_side_effects=True, vmem_limit_bytes=63 * MIB
        ),
        cost_estimate=pl.CostEstimate(flops=8 * 10**9, bytes_accessed=60 * MIB, transcendentals=0),
    )(*weights, tokens, cotangent, seq, misc)


def widen_kernel(down, gate, up, out, q, kv, y, g, o_down, o_gate, o_up, o_out, o_q, o_k, o_v, o_one, o_two, o_y, o_g):
    for a, b in ((down, o_down), (gate, o_gate), (up, o_up), (y, o_y), (g, o_g)):
        b[...] = a[...].astype(jnp.float32)
    for a, b in ((out, o_out), (q, o_q)):
        b[...] = a[:, 0:480].astype(jnp.float32)
    flipped = kv[...].astype(jnp.float32).T
    o_k[...] = flipped[0:160]
    o_v[...] = flipped[160:320]
    o_one[...] = flipped[320:321]
    o_two[...] = flipped[321:322]


def widen(sums, out, g_tok):
    f32 = jnp.float32

    def rows(n):
        return pl.BlockSpec((128, n), lambda i: (i, 0))

    def lanes(n):
        return pl.BlockSpec((n, 128), lambda i: (0, i))

    shapes = [(BLOCK, 1280)] * 3 + [(BLOCK, 480)] * 2 + [(160, BLOCK)] * 2 + [(1, BLOCK)] * 2 + [(BLOCK, 256)] * 2
    return pl.pallas_call(
        widen_kernel,
        grid=(4,),
        out_shape=[jax.ShapeDtypeStruct(s, f32) for s in shapes],
        in_specs=[rows(n) for _, n, _ in STREAMS] + [rows(256)] * 2,
        out_specs=[rows(s[1]) for s in shapes[:5]] + [lanes(160)] * 2 + [lanes(1)] * 2 + [rows(256)] * 2,
        compiler_params=pltpu.CompilerParams(vmem_limit_bytes=60 * MIB),
        cost_estimate=pl.CostEstimate(flops=0, bytes_accessed=16 * MIB, transcendentals=0),
    )(*sums, out, g_tok)


def on_device(
    tokens, gain_attn, gain_mlp, w_query, w_key, w_value, w_out, w_gate, w_up, w_down, seq_lengths, cotangent
):
    seq = jnp.pad(seq_lengths, ((0, 7), (0, 125)))
    misc = jnp.pad(jnp.stack([gain_attn, gain_mlp]), ((0, 6), (0, 32)))
    blank = jnp.zeros((BLOCK, QKV - 800), jnp.bfloat16)
    w_qkv = jnp.concatenate([w_query, w_key, w_value, blank], axis=1)
    out, g_tok, *sums = run_layer([w_qkv, w_out, w_gate, w_up, w_down], tokens, cotangent, seq, misc)
    down, gate, up, g_out, query, key, value, one, two, out, g_tok = widen(sums, out, g_tok)
    return (
        out, g_tok, one.reshape(BLOCK), two.reshape(BLOCK), query, key.T, value.T, g_out, gate, up, down
    )

def solution(mesh):
    in_specs = (
        P("row", ("tok", "col")), P("row"), P("row"), P("row", "col"), P("row", "col"), P("row", "col"),
        P("col", "row"), P("row", "col"), P("row", "col"), P("row", "col"),
        P(("tok", "row", "col"), None), P("row", ("tok", "col")),
    )
    out_specs = (
        P("row", ("tok", "col")), P("row", ("tok", "col")), P("row"), P("row"), P("row", "col"),
        P("row", "col"), P("row", "col"), P("col", "row"), P("row", "col"), P("row", "col"), P("row", "col"),
    )
    return jax.shard_map(
        on_device, mesh=mesh, in_specs=in_specs, out_specs=out_specs, check_vma=False
    )
```

```python
import math

import jax
import jax.numpy as jnp
from jax import lax
from jax.experimental import pallas as pl
from jax.experimental.pallas import tpu as pltpu
from jax.sharding import PartitionSpec as P

MESH = pl.DeviceIdType.MESH
MIB = 1024 * 1024


def position():
    t = lax.axis_index("tok")
    r = lax.axis_index("row")
    c = lax.axis_index("col")
    return {"x": (t % 2) * 2 + r, "y": (t // 2) % 4, "z": t // 8, "c": c}


def device(place, axis, step):
    p = dict(place)
    p[axis] = (p[axis] + step) % (2 if axis == "c" else 4)
    return (p["z"] * 8 + p["y"] * 2 + p["x"] // 2, p["x"] % 2, p["c"])


def meet(place):
    barrier = pltpu.get_barrier_semaphore()
    partners = [("c", 1)] + [(a, d) for a in "xyz" for d in (1, 2, 3)]
    for axis, step in partners:
        pl.semaphore_signal(
            barrier, inc=1, device_id=device(place, axis, step), device_id_type=MESH
        )
    pl.semaphore_wait(barrier, len(partners))


def send(src, dst, send_sem, recv_sem, target):
    copy = pltpu.make_async_remote_copy(
        src_ref=src, dst_ref=dst, send_sem=send_sem, recv_sem=recv_sem,
        device_id=target, device_id_type=MESH,
    )
    copy.start()
    return copy


ROWS = 512
STREAMS = (
    ("down0", 640, "xyz"),
    ("down1", 640, "xyz"),
    ("gate0", 640, "yzx"),
    ("gate1", 640, "yzx"),
    ("up0", 640, "zxy"),
    ("up1", 640, "zxy"),
    ("out", 512, "xyz"),
    ("q", 512, "yzx"),
    ("kv", 384, "zxy"),
)


def aligned(value, unit):
    return pl.multiple_of(value, unit)


class Stream:
    def __init__(self, order, place):
        self.order = order
        self.place = place

    def piece(self, acc, level, owner):
        size, start, lead = ROWS, 0, None
        for depth in range(level + 1):
            axis = self.order[depth]
            index = owner if depth == level else self.place[axis]
            if axis == "x":
                size //= 2
                start = start + (index // 2) * size
                lead = index % 2
            else:
                size //= 4
                start = start + index * size
        rows = pl.ds(aligned(start, 16), size)
        if lead is None:
            return acc.at[:, rows]
        return acc.at[lead, rows]

    def result(self, out, level):
        size, start = ROWS, 0
        for depth in range(level + 1):
            axis = self.order[depth]
            size //= 2 if axis == "x" else 4
            start = start + (self.place[axis] // 2 if axis == "x" else self.place[axis]) * size
        return out.at[pl.ds(aligned(start, 16), size)]

    def shape(self, level, n):
        size, lead = ROWS, 2
        for depth in range(level + 1):
            if self.order[depth] == "x":
                size //= 2
                lead = 1
            else:
                size //= 4
        return (lead, size, n) if lead == 2 else (size, n)


def add_rows(dst, srcs, step=16):
    shape = dst.shape
    if len(shape) == 2:
        views = [(dst, srcs)]
    else:
        views = [(dst.at[k], [s.at[k] for s in srcs]) for k in range(shape[0])]
    rows = shape[-2]
    step = min(step, rows)
    for d, ss in views:
        @pl.loop(0, rows // step)
        def _(i, d=d, ss=ss):
            at = pl.ds(aligned(i * step, step), step)
            total = d[at, :].astype(jnp.float32)
            for s in ss:
                total = total + s[at, :].astype(jnp.float32)
            d[at, :] = total.astype(d.dtype)


D = 960
HQ = 15
KVH = 5
HD = 64
EPS = 1e-05
THETA = 100000.0


def nn(left, right):
    return jnp.dot(left, right, preferred_element_type=jnp.float32)


def nt(left, right):
    return lax.dot_general(
        left, right, (((1,), (1,)), ((), ())), preferred_element_type=jnp.float32
    )


def low(value):
    return value.astype(jnp.bfloat16)


def tables(seq):
    first, second = seq[0:1, 0:1], seq[0:1, 0:1] + seq[0:1, 1:2]

    def segment(index):
        return (index >= first).astype(jnp.int32) + (index >= second).astype(jnp.int32)

    lane = lax.broadcasted_iota(jnp.int32, (1, 128), 1)
    seg_q = segment(lane)
    begin = jnp.where(seg_q == 0, 0, jnp.where(seg_q == 1, first, second))
    place = (lane - begin).astype(jnp.float32)
    ladder = lax.broadcasted_iota(jnp.int32, (32, 128), 0).astype(jnp.float32)
    angle = place * jnp.exp(ladder * (-2.0 * math.log(THETA) / HD))
    rows = lax.broadcasted_iota(jnp.int32, (128, 128), 0)
    lanes = lax.broadcasted_iota(jnp.int32, (128, 128), 1)
    seg_rows = (rows >= first).astype(jnp.int32) + (rows >= second).astype(jnp.int32)
    seg_lanes = (lanes >= first).astype(jnp.int32) + (lanes >= second).astype(jnp.int32)
    allowed = (seg_rows == seg_lanes) & (rows <= lanes)
    return jnp.cos(angle), jnp.sin(angle), allowed


def rotate(head, cosine, sine):
    a, b = head[:32], head[32:]
    return jnp.concatenate([a * cosine - b * sine, b * cosine + a * sine], axis=0)


def features_total(parts):
    return jnp.sum(parts[0], axis=0, keepdims=True) + jnp.sum(parts[1], axis=0, keepdims=True)


def inverse_rms(parts):
    return lax.rsqrt(features_total([p * p for p in parts]) / D + EPS)


def norm_back(resid, scale, gain, grad):
    weighted = [grad[r] * gain[r] for r in range(2)]
    inner = features_total([weighted[r] * resid[r] for r in range(2)]) / D
    grad_resid = [
        weighted[r] * scale - resid[r] * (scale * scale * scale * inner) for r in range(2)
    ]
    grad_gain = [jnp.sum(grad[r] * resid[r] * scale, axis=1, keepdims=True) for r in range(2)]
    return grad_resid, grad_gain

BLOCK = 480
QKV = 896
NAMES = [s[0] for s in STREAMS]
N_OF = {s[0]: s[1] for s in STREAMS}
TAIL = ("q", "kv", "down0")
ORDER = ("gate1", "up1", "down0", "gate0", "up0", "down1", "out", "q", "kv")
OWN_SPACE = NAMES[:6] + ["kv"]


def mega_kernel(*refs):
    k = 5
    src = (None,) + refs[: k - 1]
    tok, cot, w_query, w_key_t, w_value_t, lengths, gain_one_ref, gain_two_ref = refs[k - 1 : k + 7]
    refs = refs[k + 7 :]
    out_ref, g_tok_ref = refs[:2]
    result = dict(zip(NAMES, refs[2:11]))
    refs = refs[11:]
    full, refs = refs[:k], refs[k:]
    w_qkv, w_out, w_gate, w_up, w_down = full
    acc = dict(zip(OWN_SPACE, refs[:7]))
    refs = refs[7:]
    mate, refs = dict(zip(NAMES, refs[:9])), refs[9:]
    got = {name: refs[3 * i : 3 * i + 3] for i, name in enumerate(NAMES)}
    refs = refs[27:]
    (
        seq_in, seq_own, misc_all, tok_all, cot_all, n1t, flat, qkvt, q_rot, k_rot, v_rot, probs_ref,
        ctxt, midt, n2t, gate_ref, up_ref, hidden, gbt, g_gate, g_up, g_midt,
        gat, gan, g_ctx, g_qkvt, out_own, scales, cot_out, cot_low, cot_got, seq, misc,
    ) = refs[:33]
    work = qkvt.at[0:D]
    (
        local_sem, x_send, x_recv, relay_send, relay_recv, wm_send, wm_recv, act_send, act_recv,
        mate_send, mate_recv, rs_recv, ag_recv, keep_sem, end_send, end_recv, out_sem, ring_recv, last_recv,
    ) = refs[33:]
    acc["out"] = w_up.at[:, 0:ROWS, 0:512]
    acc["q"] = w_up.at[:, 0:ROWS, 512:1024]
    stage = {
        "down0": acc["gate0"].at[:, 0:BLOCK],
        "down1": acc["gate1"].at[:, 0:BLOCK],
        "gate0": w_down.at[0, :, 0:640],
        "gate1": w_down.at[0, :, 640:1280],
        "up0": w_down.at[1, :, 0:640],
        "up1": w_down.at[1, :, 640:1280],
        "out": w_gate.at[0, :, 0:512],
        "q": w_gate.at[0, :, 512:1024],
        "kv": w_gate.at[1, :, 0:384],
    }

    place = position()
    r, c = place["x"] % 2, place["c"]
    t = lax.axis_index("tok")
    row_mate, diagonal = (t, 1 - r, c), (t, 1 - r, 1 - c)
    core_mate = device(place, "c", 1)
    seq[...] = jnp.zeros((8, 128), jnp.int32)
    misc[...] = jnp.zeros((8, 512), jnp.float32)
    barrier = pltpu.get_barrier_semaphore()
    partners = [core_mate] + [device(place, a, d) for a in "xyz" for d in (1, 2, 3)] + [diagonal]
    for target in partners:
        pl.semaphore_signal(barrier, inc=1, device_id=target, device_id_type=MESH)
    pl.semaphore_wait(barrier, len(partners))

    def spot(i, row, col):
        lead, base = (row, col) if i == 1 else (col, row)
        return full[i].at[lead, pl.ds(aligned(base * BLOCK, 16), BLOCK)]

    def part(i, row, col, start, count):
        lead, base = (row, col) if i == 1 else (col, row)
        return full[i].at[lead, pl.ds(aligned(base * BLOCK + start, 16), count)]

    near, far = 1 + 2 * r, 3 - 2 * r
    x_parts = (
        (far, place["y"] * 64, 64), (near, 256 + place["z"] * 48, 48), (far, 448, 16), (near, 464, 16)
    )

    seq[0:1, 0:3] = lengths[...]
    misc[0:1, 0:BLOCK] = gain_one_ref[...]
    misc[1:2, 0:BLOCK] = gain_two_ref[...]
    seq_copy = send(seq, seq_in, act_send.at[2], act_recv.at[2], diagonal)
    misc_copy = send(misc, misc_all.at[r], act_send.at[3], act_recv.at[3], row_mate)
    theirs = pl.ds(aligned((1 - r) * 128, 128), 128)
    mine = pl.ds(aligned(r * 128, 128), 128)
    tok_copy = send(tok.at[:, theirs], tok_all.at[r], act_send.at[0], act_recv.at[0], row_mate)
    locals_ = []

    def local(a, b, sem):
        copy = pltpu.make_async_copy(a, b, sem)
        copy.start()
        return copy

    tok_local = local(tok.at[:, mine], tok_all.at[r], local_sem.at[k])
    cot_local = local(cot.at[:, mine], cot_all.at[r], local_sem.at[k + 1])
    cot_theirs = local(cot.at[:, theirs], cot_out, local_sem.at[k + 3])
    misc_local = local(misc, misc_all.at[r], local_sem.at[k + 2])
    x_in, w_local, w_mate = [], [], []

    def to_x(i, j):
        step, start, count = x_parts[j]
        own = part(0, r, c, start, count) if i == 0 else src[i].at[pl.ds(aligned(start, 16), count)]
        return send(
            own, part(i, r, c, start, count), x_send.at[i, j],
            x_recv.at[i, j], device(place, "x", step),
        )

    own_rows = pl.ds(aligned(r * BLOCK, 16), BLOCK)
    w_qkv[c, own_rows, 0:BLOCK] = w_query[...]
    w_qkv[c, own_rows, BLOCK:QKV] = jnp.concatenate(
        [w_key_t[...].T, w_value_t[...].T, jnp.zeros((BLOCK, QKV - 800), jnp.bfloat16)], axis=1
    )
    for i in range(k):
        x_in.append([to_x(i, 0), to_x(i, 1)])
        own = src[i] if i else spot(0, r, c)
        w_local.append(local(own, spot(i, r, c), local_sem.at[i]) if i else None)
        w_mate.append(send(own, spot(i, r, c), wm_send.at[i, 0], wm_recv.at[i, 0], core_mate))

    relays, forwards = {}, {}

    def pass_on(i, axis, start, count, d, slot):
        piece = part(i, 1 - r, c, start, count)
        return send(
            piece, piece, relay_send.at[i, slot], relay_recv.at[i, slot], device(place, axis, d)
        )

    def relay(i):
        x_in[i][0].wait_recv()
        relays[i] = [pass_on(i, "y", place["y"] * 64, 64, d, slot) for slot, d in ((0, 1), (1, 3))]
        x_in[i][1].wait_recv()
        relays[i] += [
            pass_on(i, "z", 256 + place["z"] * 48, 48, d, slot) for slot, d in ((2, 2), (3, 1), (4, 3))
        ]
        x_in[i] += [to_x(i, 2), to_x(i, 3)]

    def relay_on(i):
        relays[i][0].wait_recv()
        relays[i].append(pass_on(i, "y", (place["y"] + 3) % 4 * 64, 32, 1, 5))
        relays[i][1].wait_recv()
        relays[i].append(pass_on(i, "y", (place["y"] + 1) % 4 * 64 + 32, 32, 3, 6))

    def forward(i):
        for copy in x_in[i][2:] + relays[i][2:]:
            copy.wait_recv()
        block = spot(i, 1 - r, c)
        forwards[i] = send(block, block, wm_send.at[i, 1], wm_recv.at[i, 1], core_mate)

    def ready(i):
        if i:
            w_local[i].wait()
        w_mate[i].wait_recv()
        forwards[i].wait_recv()

    def release(i):
        for copy in x_in[i] + relays[i] + [w_mate[i], forwards[i]]:
            copy.wait_send()

    streams = {name: Stream(order, place) for name, _, order in STREAMS}
    mates, flying, level_of, keep = {}, {}, {}, {}

    def to_mate(name):
        i = NAMES.index(name)
        mates[name] = send(stage[name], mate[name], mate_send.at[i], mate_recv.at[i], core_mate)

    def scatter(name, level):
        i, axis = NAMES.index(name), streams[name].order[level]
        flying[name] = [
            send(
                streams[name].piece(acc[name], level, (place[axis] + d) % 4), got[name][level].at[d - 1],
                out_sem.at[i, d - 1], rs_recv.at[i, level - 1, d - 1], device(place, axis, d),
            )
            for d in (2, 1, 3)
        ]

    def spread(name, level, source=None):
        i, axis = NAMES.index(name), streams[name].order[level]
        there = streams[name].result(result[name], level)
        flying[name] = [
            send(
                there if source is None else source, there, out_sem.at[i, d - 1],
                ag_recv.at[i, level - 1, d - 1] if level else last_recv.at[i, 0, 0], device(place, axis, d),
            )
            for d in ((2,) if axis == "x" else (2, 1, 3))
        ]

    def half_of(name, owner, side):
        if streams[name].order[0] == "x":
            return acc[name].at[owner % 2, pl.ds(aligned(owner // 2 * 256 + side * 128, 16), 128)]
        return acc[name].at[side, pl.ds(aligned(owner * 128, 16), 128)]

    def ring(name, slot, source, step):
        i, axis = NAMES.index(name), streams[name].order[0]
        return send(
            source, got[name][0].at[slot], out_sem.at[i, slot], ring_recv.at[i, slot], device(place, axis, step)
        )

    def advance(name):
        step = level_of.get(name, 0)
        level_of[name] = step + 1
        i = NAMES.index(name)
        axis = streams[name].order[0]
        me = place[axis]
        after, across, before = [(me + d) % 4 for d in (1, 2, 3)]
        if step == 0:
            mates[name].wait_recv()
            for lead in range(2):
                theirs = mate[name].at[lead if name[:4] == "down" else pl.ds(lead * BLOCK, BLOCK)]
                add_rows(acc[name].at[lead, 0:BLOCK], [theirs])
            flying[name] = [
                ring(name, 0, half_of(name, across, 0), 1),
                ring(name, 1, half_of(name, across, 1), 3),
                ring(name, 2, half_of(name, after, 1), 1),
                ring(name, 3, half_of(name, before, 0), 3),
            ]
            return
        if step == 1:
            for copy, owner, side in ((flying[name][0], after, 0), (flying[name][1], before, 1)):
                copy.wait_recv()
                add_rows(half_of(name, owner, side), [got[name][0].at[side]])
            flying[name] += [
                ring(name, 4, half_of(name, after, 0), 1),
                ring(name, 5, half_of(name, before, 1), 3),
            ]
            return
        if step == 2:
            for copy in flying[name][:2]:
                copy.wait_send()
            for copy in flying[name][2:]:
                copy.wait()
            add_rows(half_of(name, me, 0), [got[name][0].at[3], got[name][0].at[4]])
            add_rows(half_of(name, me, 1), [got[name][0].at[2], got[name][0].at[5]])
            scatter(name, 1)
            return
        for copy in flying[name]:
            copy.wait()
        if step <= 4:
            level = step - 2
            own = streams[name].piece(acc[name], level, place[streams[name].order[level]])
            add_rows(own, [got[name][level].at[d] for d in range(3)])
            if level < 2:
                scatter(name, level + 1)
            else:
                keep[name] = local(own, streams[name].result(result[name], 2), keep_sem.at[i])
                spread(name, 2, own)
        elif step == 5:
            keep[name].wait()
            spread(name, 1)
        elif step == 6 and axis == "x":
            spread(name, 0)
        elif step in (6, 7) and axis != "x":
            base = [aligned(p * 128, 16) for p in (me, before, after)]
            if step == 6:
                pieces = [pl.ds(base[0], 128)] * 2
            else:
                pieces = [pl.ds(base[1], 64), pl.ds(base[2] + 64, 64)]
            flying[name] = [
                send(
                    result[name].at[rows], result[name].at[rows], out_sem.at[i, d // 2],
                    last_recv.at[i, step - 6, d // 2], device(place, axis, d),
                )
                for rows, d in zip(pieces, (1, 3))
            ]
        else:
            flying[name] = []

    def wgrad(left, right, name):
        first = 640 * int(name[-1])

        def run(col, put):
            def chunk(start, count):
                lanes = pl.ds(aligned(first + start, 128), count)
                for row in range(2):
                    rows = slice(row * BLOCK, row * BLOCK + BLOCK)
                    put(row, pl.ds(aligned(start, 128), count), low(nn(left[rows, :], right[col, :, lanes])))

            @pl.loop(0, 2)
            def _(j):
                chunk(j * 256, 256)

            chunk(512, 128)

        def put_stage(row, lanes, value):
            if name[:4] == "down":
                stage[name][row, :, lanes] = value
            else:
                stage[name][row * BLOCK : row * BLOCK + BLOCK, lanes] = value

        def put_acc(row, lanes, value):
            acc[name][row, 0:BLOCK, lanes] = value

        run(1 - c, put_stage)
        to_mate(name)
        yield
        run(c, put_acc)
        for row in range(2):
            acc[name][row, BLOCK:ROWS, :] = jnp.zeros((ROWS - BLOCK, 640), jnp.bfloat16)
        yield

    two = range(2)
    rows_of = [slice(row * BLOCK, row * BLOCK + BLOCK) for row in two]

    seq_copy.wait()
    seq_own[...] = jnp.where(r == c, seq[...], seq_in[...])
    cosine, sine, allowed = tables(seq_own[...])
    mask = jnp.concatenate([allowed] * 3, axis=1)
    misc_local.wait()
    misc_copy.wait()
    gains = [misc_all[row].T for row in two]
    gain_one = [gains[row][:BLOCK, 0:1] for row in two]
    gain_two = [gains[row][:BLOCK, 1:2] for row in two]
    tok_local.wait()
    tok_copy.wait()
    relay(0)
    relay(1)

    def resid(row):
        return tok_all[row].astype(jnp.float32)

    scales[0:1, :] = inverse_rms([resid(row) for row in two])
    for row in two:
        n1t[rows_of[row], :] = low(resid(row) * scales[0:1, :] * gain_one[row])
    flat[...] = n1t[...].T
    relay_on(0)
    relay(2)
    relay_on(1)
    relay(3)
    forward(0)
    relay(4)
    relay_on(2)
    cot_theirs.wait()
    cot_low[...] = low(cot_out[...])
    cot_copy = send(cot_low, cot_got, act_send.at[1], act_recv.at[1], row_mate)
    ready(0)
    for col in two:
        both = nn(flat[...], w_qkv[col]).T
        qkvt[col * BLOCK : col * BLOCK + BLOCK, :] = both[:BLOCK]
        qkvt[960 + col * 160 : 1120 + col * 160, :] = both[480:640]
        qkvt[1280 + col * 160 : 1440 + col * 160, :] = both[640:800]
    forward(1)
    relay_on(3)
    relay_on(4)
    for h in range(KVH):
        k_rot[h * 64 : h * 64 + 64, :] = low(rotate(qkvt[960 + h * 64 : 1024 + h * 64, :], cosine, sine))
        v_rot[h * 64 : h * 64 + 64, :] = low(qkvt[1280 + h * 64 : 1344 + h * 64, :])
        for j in range(3):
            at = (3 * h + j) * 64
            q_rot[h * 64 : h * 64 + 64, j * 128 : j * 128 + 128] = low(rotate(qkvt[at : at + 64, :], cosine, sine))
    for h in range(KVH):
        own = slice(h * 64, h * 64 + 64)
        scores = jnp.where(mask, nn(k_rot[own, :].T, q_rot[own, :]) * HD ** (-0.5), -1e30)
        expo = jnp.exp(scores - jnp.max(scores, axis=0, keepdims=True))
        probs = expo / jnp.sum(expo, axis=0, keepdims=True)
        probs_ref[h] = probs
        context = low(nn(v_rot[own, :], low(probs)))
        for j in range(3):
            at = (3 * h + j) * 64
            ctxt[at : at + 64, :] = context[:, j * 128 : j * 128 + 128]
        if h == 1:
            forward(2)
        if h == 3:
            forward(3)
    flat[...] = ctxt[...].T
    ready(1)
    for row in two:
        midt[rows_of[row], :] = resid(row) + nn(flat[...], w_out[row]).T
    forward(4)
    mids = [midt[rows_of[row], :] for row in two]
    scales[1:2, :] = inverse_rms(mids)
    for row in two:
        n2t[rows_of[row], :] = low(midt[rows_of[row], :] * scales[1:2, :] * gain_two[row])
    flat[...] = n2t[...].T
    ready(2)
    ready(3)

    @pl.loop(0, 10)
    def _(i):
        col = i // 5
        lanes = pl.ds(aligned(i % 5 * 256, 256), 256)
        gate = nn(flat[...], w_gate[col, :, lanes])
        up = nn(flat[...], w_up[col, :, lanes])
        gate_ref[col, :, lanes] = gate
        up_ref[col, :, lanes] = up
        hidden[col, :, lanes] = low(gate * jax.nn.sigmoid(gate) * up)

    cot_local.wait()
    cot_copy.wait()
    cot_all[1 - r] = cot_got[...].astype(jnp.float32)
    for row in two:
        gbt[rows_of[row], :] = low(cot_all[row])
    flat[...] = gbt[...].T
    for _ in zip(wgrad(gbt, hidden, "down0"), wgrad(gbt, hidden, "down1")):
        pass
    ready(4)

    @pl.loop(0, 10)
    def _(i):
        col = i // 5
        lanes = pl.ds(aligned(i % 5 * 256, 256), 256)
        grad = nn(flat[...], w_down[col, :, lanes])
        gate = gate_ref[col, :, lanes]
        sig = jax.nn.sigmoid(gate)
        g_gate[col, :, lanes] = low(grad * up_ref[col, :, lanes] * sig * (1.0 + gate * (1.0 - sig)))
        g_up[col, :, lanes] = low(grad * (gate * sig))

    advance("down0")
    advance("down1")
    work[...] = midt[...]
    for col in two:
        work[...] += nt(w_down[col], hidden[col])
    out_own[...] = work[...]
    out_copy = send(
        out_own.at[pl.ds(aligned((1 - r) * BLOCK, 16), BLOCK)], out_ref.at[:, mine], end_send.at[0],
        end_recv.at[0], row_mate,
    )
    out_ref[:, mine] = out_own[pl.ds(aligned(r * BLOCK, 16), BLOCK), :]
    release(4)
    mates["down0"].wait_send()
    mates["down1"].wait_send()
    works = [
        wgrad(n2t, right, name)
        for name, right in (("gate0", g_gate), ("up0", g_up), ("gate1", g_gate), ("up1", g_up))
    ]
    next(works[0])
    next(works[1])
    next(works[0])
    next(works[1])
    next(works[2])
    next(works[3])
    advance("gate0")
    advance("up0")
    next(works[2])
    next(works[3])
    advance("down0")
    work[...] = nt(w_gate[0], g_gate[0]) + nt(w_gate[1], g_gate[1])
    advance("gate1")
    advance("up1")
    work[...] += nt(w_up[0], g_up[0]) + nt(w_up[1], g_up[1])
    advance("down1")
    release(2)
    release(3)
    back, gain_two_grad = norm_back(
        [midt[rows_of[row], :] for row in two], scales[1:2, :], gain_two, [work[rows_of[row], :] for row in two]
    )
    for row in two:
        total = cot_all[row] + back[row]
        g_midt[rows_of[row], :] = total
        gat[rows_of[row], :] = low(total)
    gat[960:992, :] = jnp.zeros((32, 128), jnp.bfloat16)
    for row in two:
        gan[row] = gat[row * BLOCK : row * BLOCK + 512, :].T
    for col in two:
        at = slice(col * BLOCK, col * BLOCK + BLOCK)
        g_ctx[at, :] = low(
            nn(w_out[0, at, :], gat[0:BLOCK, :]) + nn(w_out[1, at, :], gat[BLOCK:960, :])
        )
    def out_block(col, row):
        left = ctxt[pl.ds(aligned(col * BLOCK, 16), BLOCK), :]
        return low(nn(left, gan[row]))

    for row in two:
        stage["out"][row * BLOCK : row * BLOCK + BLOCK, :] = out_block(1 - c, row)
    to_mate("out")
    for row in two:
        acc["out"][row, 0:BLOCK, :] = out_block(c, row)
        acc["out"][row, BLOCK:ROWS, :] = jnp.zeros((ROWS - BLOCK, 512), jnp.bfloat16)
    advance("gate0")
    advance("up0")
    for h in range(KVH):
        own = slice(h * 64, h * 64 + 64)
        g_cat = jnp.concatenate(
            [g_ctx[j * 64 : j * 64 + 64, :] for j in range(3 * h, 3 * h + 3)], axis=1
        )
        probs = probs_ref[h]
        g_v = low(nt(g_cat, low(probs)))
        g_probs = nn(v_rot[own, :].T, g_cat)
        g_scores = low(probs * (g_probs - jnp.sum(probs * g_probs, axis=0, keepdims=True)))
        g_q = nn(k_rot[own, :], g_scores) * HD ** (-0.5)
        g_k = low(rotate(nt(q_rot[own, :], g_scores) * HD ** (-0.5), cosine, -sine))
        parts = [(480, 160, h * 64, g_k), (640, 160, h * 64, g_v)]
        for j in range(3):
            g_j = low(rotate(g_q[:, j * 128 : j * 128 + 128], cosine, -sine))
            parts.append((0, 480, (3 * h + j) * 64, g_j))
        for base, width, at, value in parts:
            for half in two:
                row = at + 32 * half
                put = base + row % width
                g_qkvt[row // width, put : put + 32, :] = value[half * 32 : half * 32 + 32]
    for col in two:
        g_qkvt[col, 800:QKV, :] = jnp.zeros((QKV - 800, 128), jnp.bfloat16)
    advance("out")
    work[0:BLOCK, :] = nn(w_qkv[0, 0:BLOCK, :], g_qkvt[0]) + nn(w_qkv[1, 0:BLOCK, :], g_qkvt[1])
    work[BLOCK:960, :] = nn(w_qkv[0, BLOCK:960, :], g_qkvt[0]) + nn(w_qkv[1, BLOCK:960, :], g_qkvt[1])
    back, gain_one_grad = norm_back(
        [resid(row) for row in two], scales[0:1, :], gain_one, [work[rows_of[row], :] for row in two]
    )
    for row in two:
        g_midt[rows_of[row], :] = g_midt[rows_of[row], :] + back[row]
    lane = lax.broadcasted_iota(jnp.int32, (BLOCK, 384), 1)

    def q_block(col, row):
        return low(nn(n1t[rows_of[row], :], g_qkvt[col, 0:512, :].T))

    def kv_block(col, row):
        value = nn(n1t[rows_of[row], :], g_qkvt[col, 480:864, :].T)
        value = jnp.where(lane == 320, gain_one_grad[row], value)
        return low(jnp.where(lane == 321, gain_two_grad[row], value))

    for name, block, n in (("q", q_block, 512), ("kv", kv_block, 384)):
        for row in two:
            stage[name][row * BLOCK : row * BLOCK + BLOCK, :] = block(1 - c, row)
        to_mate(name)
        for row in two:
            acc[name][row, 0:BLOCK, :] = block(c, row)
            acc[name][row, BLOCK:ROWS, :] = jnp.zeros((ROWS - BLOCK, n), jnp.bfloat16)
    g_copy = send(
        g_midt.at[pl.ds(aligned((1 - r) * BLOCK, 16), BLOCK)], g_tok_ref.at[:, mine], end_send.at[1],
        end_recv.at[1], row_mate,
    )
    g_tok_ref[:, mine] = g_midt[pl.ds(aligned(r * BLOCK, 16), BLOCK), :]
    for name in TAIL:
        advance(name)
    while any(level_of[name] < 9 for name in NAMES):
        for name in ORDER:
            if level_of[name] < 9:
                advance(name)
    out_copy.wait()
    g_copy.wait()
    for name in NAMES[2:]:
        mates[name].wait_send()
    release(0)
    release(1)


def run_layer(weights, tokens, cotangent, w_query, w_key_t, w_value_t, lengths, gain_one, gain_two):
    bf, f32 = jnp.bfloat16, jnp.float32
    dma = pltpu.SemaphoreType.DMA
    hbm, vmem = pl.BlockSpec(memory_space=pl.ANY), pl.BlockSpec(memory_space=pltpu.VMEM)
    place = {"x": 0, "y": 0, "z": 0, "c": 0}

    def v(shape, dtype=bf):
        return pltpu.VMEM(shape, dtype)

    scratch = [v((2, 2 * BLOCK, QKV))] + [v((2, 2 * BLOCK, w.shape[1])) for w in weights]
    scratch += [v((2, ROWS, N_OF[name])) for name in OWN_SPACE]
    scratch += [v((2, BLOCK, n) if name[:4] == "down" else (2 * BLOCK, n)) for name, n, _ in STREAMS]
    for _, n, order in STREAMS:
        for level in range(3):
            scratch.append(v((3,) + Stream(order, place).shape(level, n) if level else (6, 128, n)))
    scratch += [
        v((8, 128), jnp.int32), v((8, 128), jnp.int32), v((2, 8, 512), f32), v((2, BLOCK, 128)),
        v((2, BLOCK, 128), f32), v((D, 128)), v((128, D)), v((1600, 128), f32), v((320, 384)),
        v((320, 128)), v((320, 128)), v((KVH, 128, 384), f32), v((D, 128)), v((D, 128), f32),
        v((D, 128)), v((2, 128, 1280), f32), v((2, 128, 1280), f32), v((2, 128, 1280)),
        v((D, 128)), v((2, 128, 1280)), v((2, 128, 1280)),
        v((D, 128), f32), v((992, 128)), v((2, 128, 512)), v((D, 128)), v((2, QKV, 128)), v((D, 128), f32),
        v((8, 128), f32), v((BLOCK, 128), f32), v((BLOCK, 128)), v((BLOCK, 128)), v((8, 128), jnp.int32),
        v((8, 512), f32),
    ]
    scratch += [
        dma((9,)), dma((5, 4)), dma((5, 4)), dma((5, 7)), dma((5, 7)), dma((5, 2)), dma((5, 2)),
        dma((4,)), dma((4,)), dma((9,)), dma((9,)), dma((9, 2, 3)), dma((9, 2, 3)), dma((9,)), dma((2,)), dma((2,)),
        dma((9, 6)), dma((9, 6)), dma((9, 2, 2)),
    ]
    return pl.pallas_call(
        mega_kernel,
        out_shape=[jax.ShapeDtypeStruct((BLOCK, 256), f32)] * 2
        + [jax.ShapeDtypeStruct((ROWS, n), bf) for _, n, _ in STREAMS],
        in_specs=[hbm] * 6 + [vmem] * 6,
        out_specs=[vmem] * 2 + [hbm] * 9,
        scratch_shapes=scratch,
        compiler_params=pltpu.CompilerParams(
            collective_id=1, has_side_effects=True, vmem_limit_bytes=63 * MIB
        ),
        cost_estimate=pl.CostEstimate(flops=8 * 10**9, bytes_accessed=60 * MIB, transcendentals=0),
    )(*weights, tokens, cotangent, w_query, w_key_t, w_value_t, lengths, gain_one, gain_two)


def widen_kernel(
    down0, down1, gate0, gate1, up0, up1, out, q, kv, y, g,
    o_down, o_gate, o_up, o_out, o_q, o_k, o_v, o_one, o_two, o_y, o_g
):
    for a, b, whole in ((down0, down1, o_down), (gate0, gate1, o_gate), (up0, up1, o_up)):
        whole[:, 0:640] = a[...].astype(jnp.float32)
        whole[:, 640:1280] = b[...].astype(jnp.float32)
    o_y[...] = y[...]
    o_g[...] = g[...]
    for a, b in ((out, o_out), (q, o_q)):
        b[...] = a[:, 0:480].astype(jnp.float32)
    flipped = kv[...].astype(jnp.float32).T
    o_k[...] = flipped[0:160]
    o_v[...] = flipped[160:320]
    o_one[...] = flipped[320:321]
    o_two[...] = flipped[321:322]


def widen(sums, out, g_tok):
    f32 = jnp.float32

    def rows(n):
        return pl.BlockSpec((128, n), lambda i: (i, 0))

    def lanes(n):
        return pl.BlockSpec((n, 128), lambda i: (0, i))

    shapes = [(BLOCK, 1280)] * 3 + [(BLOCK, 480)] * 2 + [(160, BLOCK)] * 2 + [(1, BLOCK)] * 2 + [(BLOCK, 256)] * 2
    return pl.pallas_call(
        widen_kernel,
        grid=(4,),
        out_shape=[jax.ShapeDtypeStruct(s, f32) for s in shapes],
        in_specs=[rows(n) for _, n, _ in STREAMS] + [rows(256)] * 2,
        out_specs=[rows(s[1]) for s in shapes[:5]] + [lanes(160)] * 2 + [lanes(1)] * 2 + [rows(256)] * 2,
        compiler_params=pltpu.CompilerParams(vmem_limit_bytes=60 * MIB),
        cost_estimate=pl.CostEstimate(flops=0, bytes_accessed=16 * MIB, transcendentals=0),
    )(*sums, out, g_tok)


def on_device(
    tokens, gain_attn, gain_mlp, w_query, w_key, w_value, w_out, w_gate, w_up, w_down, seq_lengths, cotangent
):
    out, g_tok, *sums = run_layer(
        [w_out, w_gate, w_up, w_down], tokens, cotangent, w_query, w_key.T, w_value.T, seq_lengths,
        gain_attn.reshape(1, BLOCK), gain_mlp.reshape(1, BLOCK),
    )
    down, gate, up, g_out, query, key, value, one, two, out, g_tok = widen(sums, out, g_tok)
    return (
        out, g_tok, one.reshape(BLOCK), two.reshape(BLOCK), query, key.T, value.T, g_out, gate, up, down
    )

def solution(mesh):
    in_specs = (
        P("row", ("tok", "col")), P("row"), P("row"), P("row", "col"), P("row", "col"), P("row", "col"),
        P("col", "row"), P("row", "col"), P("row", "col"), P("row", "col"),
        P(("tok", "row", "col"), None), P("row", ("tok", "col")),
    )
    out_specs = (
        P("row", ("tok", "col")), P("row", ("tok", "col")), P("row"), P("row"), P("row", "col"),
        P("row", "col"), P("row", "col"), P("col", "row"), P("row", "col"), P("row", "col"), P("row", "col"),
    )
    return jax.shard_map(
        on_device, mesh=mesh, in_specs=in_specs, out_specs=out_specs, check_vma=False
    )
```

```python
import math

import jax
import jax.numpy as jnp
from jax import lax
from jax.experimental import pallas as pl
from jax.experimental.pallas import tpu as pltpu
from jax.sharding import PartitionSpec as P

MESH = pl.DeviceIdType.MESH
MIB = 1024 * 1024


def position():
    t = lax.axis_index("tok")
    r = lax.axis_index("row")
    c = lax.axis_index("col")
    return {"x": (t % 2) * 2 + r, "y": (t // 2) % 4, "z": t // 8, "c": c}


def device(place, axis, step):
    p = dict(place)
    p[axis] = (p[axis] + step) % (2 if axis == "c" else 4)
    return (p["z"] * 8 + p["y"] * 2 + p["x"] // 2, p["x"] % 2, p["c"])


def meet(place):
    barrier = pltpu.get_barrier_semaphore()
    partners = [("c", 1)] + [(a, d) for a in "xyz" for d in (1, 2, 3)]
    for axis, step in partners:
        pl.semaphore_signal(
            barrier, inc=1, device_id=device(place, axis, step), device_id_type=MESH
        )
    pl.semaphore_wait(barrier, len(partners))


def send(src, dst, send_sem, recv_sem, target):
    copy = pltpu.make_async_remote_copy(
        src_ref=src, dst_ref=dst, send_sem=send_sem, recv_sem=recv_sem,
        device_id=target, device_id_type=MESH,
    )
    copy.start()
    return copy


ROWS = 512
STREAMS = (
    ("down0", 640, "xyz"),
    ("down1", 640, "xyz"),
    ("gate0", 640, "yzx"),
    ("gate1", 640, "yzx"),
    ("up0", 640, "zxy"),
    ("up1", 640, "zxy"),
    ("out", 512, "xyz"),
    ("q", 512, "yzx"),
    ("kv", 384, "zxy"),
)


def aligned(value, unit):
    return pl.multiple_of(value, unit)


class Stream:
    def __init__(self, order, place):
        self.order = order
        self.place = place

    def piece(self, acc, level, owner):
        size, start, lead = ROWS, 0, None
        for depth in range(level + 1):
            axis = self.order[depth]
            index = owner if depth == level else self.place[axis]
            if axis == "x":
                size //= 2
                start = start + (index // 2) * size
                lead = index % 2
            else:
                size //= 4
                start = start + index * size
        rows = pl.ds(aligned(start, 16), size)
        if lead is None:
            return acc.at[:, rows]
        return acc.at[lead, rows]

    def result(self, out, level):
        size, start = ROWS, 0
        for depth in range(level + 1):
            axis = self.order[depth]
            size //= 2 if axis == "x" else 4
            start = start + (self.place[axis] // 2 if axis == "x" else self.place[axis]) * size
        return out.at[pl.ds(aligned(start, 16), size)]

    def shape(self, level, n):
        size, lead = ROWS, 2
        for depth in range(level + 1):
            if self.order[depth] == "x":
                size //= 2
                lead = 1
            else:
                size //= 4
        return (lead, size, n) if lead == 2 else (size, n)


def add_rows(dst, srcs, step=32):
    shape = dst.shape
    if len(shape) == 2:
        views = [(dst, srcs)]
    else:
        views = [(dst.at[k], [s.at[k] for s in srcs]) for k in range(shape[0])]
    rows = shape[-2]
    step = min(step, rows)
    for d, ss in views:
        @pl.loop(0, rows // step)
        def _(i, d=d, ss=ss):
            at = pl.ds(aligned(i * step, step), step)
            if len(ss) == 1:
                d[at, :] = d[at, :] + ss[0][at, :]
                return
            total = d[at, :].astype(jnp.float32)
            for s in ss:
                total = total + s[at, :].astype(jnp.float32)
            d[at, :] = total.astype(d.dtype)


D = 960
HQ = 15
KVH = 5
HD = 64
EPS = 1e-05
THETA = 100000.0


def nn(left, right):
    return jnp.dot(left, right, preferred_element_type=jnp.float32)


def nt(left, right):
    return lax.dot_general(
        left, right, (((1,), (1,)), ((), ())), preferred_element_type=jnp.float32
    )


def low(value):
    return value.astype(jnp.bfloat16)


def tables(seq):
    first, second = seq[0:1, 0:1], seq[0:1, 0:1] + seq[0:1, 1:2]

    def segment(index):
        return (index >= first).astype(jnp.int32) + (index >= second).astype(jnp.int32)

    lane = lax.broadcasted_iota(jnp.int32, (1, 128), 1)
    seg_q = segment(lane)
    begin = jnp.where(seg_q == 0, 0, jnp.where(seg_q == 1, first, second))
    place = (lane - begin).astype(jnp.float32)
    ladder = lax.broadcasted_iota(jnp.int32, (32, 128), 0).astype(jnp.float32)
    angle = place * jnp.exp(ladder * (-2.0 * math.log(THETA) / HD))
    rows = lax.broadcasted_iota(jnp.int32, (128, 128), 0)
    lanes = lax.broadcasted_iota(jnp.int32, (128, 128), 1)
    seg_rows = (rows >= first).astype(jnp.int32) + (rows >= second).astype(jnp.int32)
    seg_lanes = (lanes >= first).astype(jnp.int32) + (lanes >= second).astype(jnp.int32)
    allowed = (seg_rows == seg_lanes) & (rows <= lanes)
    return jnp.cos(angle), jnp.sin(angle), allowed


def rotate(head, cosine, sine):
    a, b = head[:32], head[32:]
    return jnp.concatenate([a * cosine - b * sine, b * cosine + a * sine], axis=0)


def features_total(parts):
    return jnp.sum(parts[0], axis=0, keepdims=True) + jnp.sum(parts[1], axis=0, keepdims=True)


def inverse_rms(parts):
    return lax.rsqrt(features_total([p * p for p in parts]) / D + EPS)


def norm_back(resid, scale, gain, grad):
    weighted = [grad[r] * gain[r] for r in range(2)]
    inner = features_total([weighted[r] * resid[r] for r in range(2)]) / D
    grad_resid = [
        weighted[r] * scale - resid[r] * (scale * scale * scale * inner) for r in range(2)
    ]
    grad_gain = [jnp.sum(grad[r] * resid[r] * scale, axis=1, keepdims=True) for r in range(2)]
    return grad_resid, grad_gain

BLOCK = 480
QKV = 896
NAMES = [s[0] for s in STREAMS]
N_OF = {s[0]: s[1] for s in STREAMS}
TAIL = ("down0", "q", "kv")
ORDER = ("gate1", "up1", "down0", "gate0", "up0", "down1", "out", "q", "kv")
OWN_SPACE = NAMES[:6] + ["kv"]


def mega_kernel(*refs):
    k = 5
    src = (None,) + refs[: k - 1]
    tok, cot, w_query, w_key_t, w_value_t, lengths, gain_one_ref, gain_two_ref = refs[k - 1 : k + 7]
    refs = refs[k + 7 :]
    out_ref, g_tok_ref = refs[:2]
    result = dict(zip(NAMES, refs[2:11]))
    refs = refs[11:]
    full, refs = refs[:k], refs[k:]
    w_qkv, w_out, w_gate, w_up, w_down = full
    acc = dict(zip(OWN_SPACE, refs[:7]))
    refs = refs[7:]
    mate, refs = dict(zip(NAMES, refs[:9])), refs[9:]
    got = {name: refs[3 * i : 3 * i + 3] for i, name in enumerate(NAMES)}
    refs = refs[27:]
    (
        seq_in, seq_own, misc_all, tok_all, cot_all, n1t, flat, qkvt, q_rot, k_rot, v_rot, probs_ref,
        ctxt, midt, n2t, gate_ref, up_ref, hidden, gbt, g_gate, g_up, g_midt,
        gat, gan, g_ctx, g_qkvt, out_own, scales, cot_out, cot_low, cot_got, seq, misc,
    ) = refs[:33]
    work = qkvt.at[0:D]
    (
        local_sem, x_send, x_recv, relay_send, relay_recv, wm_send, wm_recv, act_send, act_recv,
        mate_send, mate_recv, rs_recv, ag_recv, keep_sem, end_send, end_recv, out_sem, ring_recv, last_recv,
    ) = refs[33:]
    acc["out"] = w_up.at[:, 0:ROWS, 0:512]
    acc["q"] = w_up.at[:, 0:ROWS, 512:1024]
    stage = {
        "down0": acc["gate0"].at[:, 0:BLOCK],
        "down1": acc["gate1"].at[:, 0:BLOCK],
        "gate0": w_down.at[0, :, 0:640],
        "gate1": w_down.at[0, :, 640:1280],
        "up0": w_down.at[1, :, 0:640],
        "up1": w_down.at[1, :, 640:1280],
        "out": w_gate.at[0, :, 0:512],
        "q": w_gate.at[0, :, 512:1024],
        "kv": w_gate.at[1, :, 0:384],
    }

    place = position()
    r, c = place["x"] % 2, place["c"]
    t = lax.axis_index("tok")
    row_mate, diagonal = (t, 1 - r, c), (t, 1 - r, 1 - c)
    core_mate = device(place, "c", 1)
    seq[...] = jnp.zeros((8, 128), jnp.int32)
    misc[...] = jnp.zeros((8, 512), jnp.float32)
    barrier = pltpu.get_barrier_semaphore()
    partners = [core_mate] + [device(place, a, d) for a in "xyz" for d in (1, 2, 3)] + [diagonal]
    for target in partners:
        pl.semaphore_signal(barrier, inc=1, device_id=target, device_id_type=MESH)
    pl.semaphore_wait(barrier, len(partners))

    def spot(i, row, col):
        lead, base = (row, col) if i == 1 else (col, row)
        return full[i].at[lead, pl.ds(aligned(base * BLOCK, 16), BLOCK)]

    def part(i, row, col, start, count):
        lead, base = (row, col) if i == 1 else (col, row)
        return full[i].at[lead, pl.ds(aligned(base * BLOCK + start, 16), count)]

    near, far = 1 + 2 * r, 3 - 2 * r
    x_parts = (
        (far, place["y"] * 64, 64), (near, 256 + place["z"] * 48, 48), (far, 448, 16), (near, 464, 16)
    )

    seq[0:1, 0:3] = lengths[...]
    misc[0:1, 0:BLOCK] = gain_one_ref[...]
    misc[1:2, 0:BLOCK] = gain_two_ref[...]
    seq_copy = send(seq, seq_in, act_send.at[2], act_recv.at[2], diagonal)
    misc_copy = send(misc, misc_all.at[r], act_send.at[3], act_recv.at[3], row_mate)
    theirs = pl.ds(aligned((1 - r) * 128, 128), 128)
    mine = pl.ds(aligned(r * 128, 128), 128)
    tok_copy = send(tok.at[:, theirs], tok_all.at[r], act_send.at[0], act_recv.at[0], row_mate)
    locals_ = []

    def local(a, b, sem):
        copy = pltpu.make_async_copy(a, b, sem)
        copy.start()
        return copy

    tok_local = local(tok.at[:, mine], tok_all.at[r], local_sem.at[k])
    cot_local = local(cot.at[:, mine], cot_all.at[r], local_sem.at[k + 1])
    cot_theirs = local(cot.at[:, theirs], cot_out, local_sem.at[k + 3])
    misc_local = local(misc, misc_all.at[r], local_sem.at[k + 2])
    x_in, w_local, w_mate = [], [], []

    def to_x(i, j):
        step, start, count = x_parts[j]
        own = part(0, r, c, start, count) if i == 0 else src[i].at[pl.ds(aligned(start, 16), count)]
        return send(
            own, part(i, r, c, start, count), x_send.at[i, j],
            x_recv.at[i, j], device(place, "x", step),
        )

    own_rows = pl.ds(aligned(r * BLOCK, 16), BLOCK)
    w_qkv[c, own_rows, 0:BLOCK] = w_query[...]
    w_qkv[c, own_rows, BLOCK:QKV] = jnp.concatenate(
        [w_key_t[...].T, w_value_t[...].T, jnp.zeros((BLOCK, QKV - 800), jnp.bfloat16)], axis=1
    )
    for i in range(k):
        x_in.append([to_x(i, 0), to_x(i, 1)])
        own = src[i] if i else spot(0, r, c)
        w_local.append(local(own, spot(i, r, c), local_sem.at[i]) if i else None)
        w_mate.append(send(own, spot(i, r, c), wm_send.at[i, 0], wm_recv.at[i, 0], core_mate))

    relays, forwards = {}, {}

    def pass_on(i, axis, start, count, d, slot):
        piece = part(i, 1 - r, c, start, count)
        return send(
            piece, piece, relay_send.at[i, slot], relay_recv.at[i, slot], device(place, axis, d)
        )

    def relay(i):
        x_in[i][0].wait_recv()
        relays[i] = [pass_on(i, "y", place["y"] * 64, 64, d, slot) for slot, d in ((0, 1), (1, 3))]
        x_in[i][1].wait_recv()
        relays[i] += [
            pass_on(i, "z", 256 + place["z"] * 48, 48, d, slot) for slot, d in ((2, 2), (3, 1), (4, 3))
        ]
        x_in[i] += [to_x(i, 2), to_x(i, 3)]

    def relay_on(i):
        relays[i][0].wait_recv()
        relays[i].append(pass_on(i, "y", (place["y"] + 3) % 4 * 64, 32, 1, 5))
        relays[i][1].wait_recv()
        relays[i].append(pass_on(i, "y", (place["y"] + 1) % 4 * 64 + 32, 32, 3, 6))

    def forward(i):
        for copy in x_in[i][2:] + relays[i][2:]:
            copy.wait_recv()
        block = spot(i, 1 - r, c)
        forwards[i] = send(block, block, wm_send.at[i, 1], wm_recv.at[i, 1], core_mate)

    def ready(i):
        if i:
            w_local[i].wait()
        w_mate[i].wait_recv()
        forwards[i].wait_recv()

    def release(i):
        for copy in x_in[i] + relays[i] + [w_mate[i], forwards[i]]:
            copy.wait_send()

    streams = {name: Stream(order, place) for name, _, order in STREAMS}
    mates, flying, level_of, keep = {}, {}, {}, {}

    def to_mate(name):
        i = NAMES.index(name)
        mates[name] = send(stage[name], mate[name], mate_send.at[i], mate_recv.at[i], core_mate)

    def scatter(name, level):
        i, axis = NAMES.index(name), streams[name].order[level]
        flying[name] = [
            send(
                streams[name].piece(acc[name], level, (place[axis] + d) % 4), got[name][level].at[d - 1],
                out_sem.at[i, d - 1], rs_recv.at[i, level - 1, d - 1], device(place, axis, d),
            )
            for d in (2, 1, 3)
        ]

    def spread(name, level, source=None):
        i, axis = NAMES.index(name), streams[name].order[level]
        there = streams[name].result(result[name], level)
        flying[name] = [
            send(
                there if source is None else source, there, out_sem.at[i, d - 1],
                ag_recv.at[i, level - 1, d - 1] if level else last_recv.at[i, 0, 0], device(place, axis, d),
            )
            for d in ((2,) if axis == "x" else (2, 1, 3))
        ]

    def half_of(name, owner, side):
        if streams[name].order[0] == "x":
            return acc[name].at[owner % 2, pl.ds(aligned(owner // 2 * 256 + side * 128, 16), 128)]
        return acc[name].at[side, pl.ds(aligned(owner * 128, 16), 128)]

    def ring(name, slot, source, step):
        i, axis = NAMES.index(name), streams[name].order[0]
        return send(
            source, got[name][0].at[slot], out_sem.at[i, slot], ring_recv.at[i, slot], device(place, axis, step)
        )

    def advance(name):
        step = level_of.get(name, 0)
        level_of[name] = step + 1
        i = NAMES.index(name)
        axis = streams[name].order[0]
        me = place[axis]
        after, across, before = [(me + d) % 4 for d in (1, 2, 3)]
        if step == 0:
            mates[name].wait_recv()
            for lead in range(2):
                theirs = mate[name].at[lead if name[:4] == "down" else pl.ds(lead * BLOCK, BLOCK)]
                add_rows(acc[name].at[lead, 0:BLOCK], [theirs])
            flying[name] = [
                ring(name, 0, half_of(name, across, 0), 1),
                ring(name, 1, half_of(name, across, 1), 3),
                ring(name, 2, half_of(name, after, 1), 1),
                ring(name, 3, half_of(name, before, 0), 3),
            ]
            return
        if step == 1:
            for copy, owner, side in ((flying[name][0], after, 0), (flying[name][1], before, 1)):
                copy.wait_recv()
                add_rows(half_of(name, owner, side), [got[name][0].at[side]])
            flying[name] += [
                ring(name, 4, half_of(name, after, 0), 1),
                ring(name, 5, half_of(name, before, 1), 3),
            ]
            return
        if step == 2:
            for copy in flying[name][:2]:
                copy.wait_send()
            for copy in flying[name][2:]:
                copy.wait()
            add_rows(half_of(name, me, 0), [got[name][0].at[3], got[name][0].at[4]])
            add_rows(half_of(name, me, 1), [got[name][0].at[2], got[name][0].at[5]])
            scatter(name, 1)
            return
        for copy in flying[name]:
            copy.wait()
        if step <= 4:
            level = step - 2
            own = streams[name].piece(acc[name], level, place[streams[name].order[level]])
            add_rows(own, [got[name][level].at[d] for d in range(3)])
            if level < 2:
                scatter(name, level + 1)
            else:
                keep[name] = local(own, streams[name].result(result[name], 2), keep_sem.at[i])
                spread(name, 2, own)
        elif step == 5:
            keep[name].wait()
            spread(name, 1)
        elif step == 6 and axis == "x":
            spread(name, 0)
        elif step in (6, 7) and axis != "x":
            base = [aligned(p * 128, 16) for p in (me, before, after)]
            if step == 6:
                pieces = [pl.ds(base[0], 128)] * 2
            else:
                pieces = [pl.ds(base[1], 64), pl.ds(base[2] + 64, 64)]
            flying[name] = [
                send(
                    result[name].at[rows], result[name].at[rows], out_sem.at[i, d // 2],
                    last_recv.at[i, step - 6, d // 2], device(place, axis, d),
                )
                for rows, d in zip(pieces, (1, 3))
            ]
        else:
            flying[name] = []

    def wgrad(left, right, name):
        first = 640 * int(name[-1])

        def run(col, put):
            def chunk(start, count):
                lanes = pl.ds(aligned(first + start, 128), count)
                for row in range(2):
                    rows = slice(row * BLOCK, row * BLOCK + BLOCK)
                    put(row, pl.ds(aligned(start, 128), count), low(nn(left[rows, :], right[col, :, lanes])))

            @pl.loop(0, 2)
            def _(j):
                chunk(j * 256, 256)

            chunk(512, 128)

        def put_stage(row, lanes, value):
            if name[:4] == "down":
                stage[name][row, :, lanes] = value
            else:
                stage[name][row * BLOCK : row * BLOCK + BLOCK, lanes] = value

        def put_acc(row, lanes, value):
            acc[name][row, 0:BLOCK, lanes] = value

        run(1 - c, put_stage)
        to_mate(name)
        yield
        run(c, put_acc)
        for row in range(2):
            acc[name][row, BLOCK:ROWS, :] = jnp.zeros((ROWS - BLOCK, 640), jnp.bfloat16)
        yield

    two = range(2)
    rows_of = [slice(row * BLOCK, row * BLOCK + BLOCK) for row in two]

    seq_copy.wait()
    seq_own[...] = jnp.where(r == c, seq[...], seq_in[...])
    cosine, sine, allowed = tables(seq_own[...])
    mask = jnp.concatenate([allowed] * 3, axis=1)
    misc_local.wait()
    misc_copy.wait()
    gains = [misc_all[row].T for row in two]
    gain_one = [gains[row][:BLOCK, 0:1] for row in two]
    gain_two = [gains[row][:BLOCK, 1:2] for row in two]
    tok_local.wait()
    tok_copy.wait()
    relay(0)
    relay(1)

    def resid(row):
        return tok_all[row].astype(jnp.float32)

    scales[0:1, :] = inverse_rms([resid(row) for row in two])
    for row in two:
        n1t[rows_of[row], :] = low(resid(row) * scales[0:1, :] * gain_one[row])
    flat[...] = n1t[...].T
    relay_on(0)
    relay(2)
    relay_on(1)
    relay(3)
    forward(0)
    relay(4)
    relay_on(2)
    cot_theirs.wait()
    cot_low[...] = low(cot_out[...])
    cot_copy = send(cot_low, cot_got, act_send.at[1], act_recv.at[1], row_mate)
    ready(0)
    for col in two:
        both = nn(flat[...], w_qkv[col]).T
        qkvt[col * BLOCK : col * BLOCK + BLOCK, :] = both[:BLOCK]
        qkvt[960 + col * 160 : 1120 + col * 160, :] = both[480:640]
        qkvt[1280 + col * 160 : 1440 + col * 160, :] = both[640:800]
    forward(1)
    relay_on(3)
    relay_on(4)
    for h in range(KVH):
        k_rot[h * 64 : h * 64 + 64, :] = low(rotate(qkvt[960 + h * 64 : 1024 + h * 64, :], cosine, sine))
        v_rot[h * 64 : h * 64 + 64, :] = low(qkvt[1280 + h * 64 : 1344 + h * 64, :])
        for j in range(3):
            at = (3 * h + j) * 64
            q_rot[h * 64 : h * 64 + 64, j * 128 : j * 128 + 128] = low(rotate(qkvt[at : at + 64, :], cosine, sine))
    for h in range(KVH):
        own = slice(h * 64, h * 64 + 64)
        scores = jnp.where(mask, nn(k_rot[own, :].T, q_rot[own, :]) * HD ** (-0.5), -1e30)
        expo = jnp.exp(scores - jnp.max(scores, axis=0, keepdims=True))
        probs = expo / jnp.sum(expo, axis=0, keepdims=True)
        probs_ref[h] = probs
        context = low(nn(v_rot[own, :], low(probs)))
        for j in range(3):
            at = (3 * h + j) * 64
            ctxt[at : at + 64, :] = context[:, j * 128 : j * 128 + 128]
        if h == 1:
            forward(2)
        if h == 3:
            forward(3)
    flat[...] = ctxt[...].T
    ready(1)
    for row in two:
        midt[rows_of[row], :] = resid(row) + nn(flat[...], w_out[row]).T
    forward(4)
    mids = [midt[rows_of[row], :] for row in two]
    scales[1:2, :] = inverse_rms(mids)
    for row in two:
        n2t[rows_of[row], :] = low(midt[rows_of[row], :] * scales[1:2, :] * gain_two[row])
    flat[...] = n2t[...].T
    ready(2)
    ready(3)

    @pl.loop(0, 10)
    def _(i):
        col = i // 5
        lanes = pl.ds(aligned(i % 5 * 256, 256), 256)
        gate = nn(flat[...], w_gate[col, :, lanes])
        up = nn(flat[...], w_up[col, :, lanes])
        gate_ref[col, :, lanes] = gate
        up_ref[col, :, lanes] = up
        hidden[col, :, lanes] = low(gate * jax.nn.sigmoid(gate) * up)

    cot_local.wait()
    cot_copy.wait()
    cot_all[1 - r] = cot_got[...].astype(jnp.float32)
    for row in two:
        gbt[rows_of[row], :] = low(cot_all[row])
    flat[...] = gbt[...].T
    for _ in zip(wgrad(gbt, hidden, "down0"), wgrad(gbt, hidden, "down1")):
        pass
    ready(4)

    @pl.loop(0, 10)
    def _(i):
        col = i // 5
        lanes = pl.ds(aligned(i % 5 * 256, 256), 256)
        grad = nn(flat[...], w_down[col, :, lanes])
        gate = gate_ref[col, :, lanes]
        sig = jax.nn.sigmoid(gate)
        g_gate[col, :, lanes] = low(grad * up_ref[col, :, lanes] * sig * (1.0 + gate * (1.0 - sig)))
        g_up[col, :, lanes] = low(grad * (gate * sig))

    advance("down0")
    advance("down1")
    work[...] = midt[...]
    for col in two:
        work[...] += nt(w_down[col], hidden[col])
    out_own[...] = work[...]
    out_copy = send(
        out_own.at[pl.ds(aligned((1 - r) * BLOCK, 16), BLOCK)], out_ref.at[:, mine], end_send.at[0],
        end_recv.at[0], row_mate,
    )
    out_ref[:, mine] = out_own[pl.ds(aligned(r * BLOCK, 16), BLOCK), :]
    release(4)
    mates["down0"].wait_send()
    mates["down1"].wait_send()
    works = [
        wgrad(n2t, right, name)
        for name, right in (("gate0", g_gate), ("up0", g_up), ("gate1", g_gate), ("up1", g_up))
    ]
    next(works[0])
    next(works[1])
    next(works[0])
    next(works[1])
    next(works[2])
    next(works[3])
    advance("gate0")
    advance("up0")
    next(works[2])
    next(works[3])
    advance("down0")
    work[...] = nt(w_gate[0], g_gate[0]) + nt(w_gate[1], g_gate[1])
    advance("gate1")
    advance("up1")
    work[...] += nt(w_up[0], g_up[0]) + nt(w_up[1], g_up[1])
    advance("down1")
    release(2)
    release(3)
    back, gain_two_grad = norm_back(
        [midt[rows_of[row], :] for row in two], scales[1:2, :], gain_two, [work[rows_of[row], :] for row in two]
    )
    for row in two:
        total = cot_all[row] + back[row]
        g_midt[rows_of[row], :] = total
        gat[rows_of[row], :] = low(total)
    gat[960:992, :] = jnp.zeros((32, 128), jnp.bfloat16)
    for row in two:
        gan[row] = gat[row * BLOCK : row * BLOCK + 512, :].T
    for col in two:
        at = slice(col * BLOCK, col * BLOCK + BLOCK)
        g_ctx[at, :] = low(
            nn(w_out[0, at, :], gat[0:BLOCK, :]) + nn(w_out[1, at, :], gat[BLOCK:960, :])
        )
    def out_block(col, row):
        left = ctxt[pl.ds(aligned(col * BLOCK, 16), BLOCK), :]
        return low(nn(left, gan[row]))

    for row in two:
        stage["out"][row * BLOCK : row * BLOCK + BLOCK, :] = out_block(1 - c, row)
    to_mate("out")
    for row in two:
        acc["out"][row, 0:BLOCK, :] = out_block(c, row)
        acc["out"][row, BLOCK:ROWS, :] = jnp.zeros((ROWS - BLOCK, 512), jnp.bfloat16)
    advance("gate0")
    advance("up0")
    for h in range(KVH):
        own = slice(h * 64, h * 64 + 64)
        g_cat = jnp.concatenate(
            [g_ctx[j * 64 : j * 64 + 64, :] for j in range(3 * h, 3 * h + 3)], axis=1
        )
        probs = probs_ref[h]
        g_v = low(nt(g_cat, low(probs)))
        g_probs = nn(v_rot[own, :].T, g_cat)
        g_scores = low(probs * (g_probs - jnp.sum(probs * g_probs, axis=0, keepdims=True)))
        g_q = nn(k_rot[own, :], g_scores) * HD ** (-0.5)
        g_k = low(rotate(nt(q_rot[own, :], g_scores) * HD ** (-0.5), cosine, -sine))
        parts = [(480, 160, h * 64, g_k), (640, 160, h * 64, g_v)]
        for j in range(3):
            g_j = low(rotate(g_q[:, j * 128 : j * 128 + 128], cosine, -sine))
            parts.append((0, 480, (3 * h + j) * 64, g_j))
        for base, width, at, value in parts:
            for half in two:
                row = at + 32 * half
                put = base + row % width
                g_qkvt[row // width, put : put + 32, :] = value[half * 32 : half * 32 + 32]
    for col in two:
        g_qkvt[col, 800:QKV, :] = jnp.zeros((QKV - 800, 128), jnp.bfloat16)
    advance("out")
    work[0:BLOCK, :] = nn(w_qkv[0, 0:BLOCK, :], g_qkvt[0]) + nn(w_qkv[1, 0:BLOCK, :], g_qkvt[1])
    work[BLOCK:960, :] = nn(w_qkv[0, BLOCK:960, :], g_qkvt[0]) + nn(w_qkv[1, BLOCK:960, :], g_qkvt[1])
    back, gain_one_grad = norm_back(
        [resid(row) for row in two], scales[0:1, :], gain_one, [work[rows_of[row], :] for row in two]
    )
    for row in two:
        g_midt[rows_of[row], :] = g_midt[rows_of[row], :] + back[row]
    lane = lax.broadcasted_iota(jnp.int32, (BLOCK, 384), 1)

    def q_block(col, row):
        return low(nn(n1t[rows_of[row], :], g_qkvt[col, 0:512, :].T))

    def kv_block(col, row):
        value = nn(n1t[rows_of[row], :], g_qkvt[col, 480:864, :].T)
        value = jnp.where(lane == 320, gain_one_grad[row], value)
        return low(jnp.where(lane == 321, gain_two_grad[row], value))

    for name, block, n in (("q", q_block, 512), ("kv", kv_block, 384)):
        for row in two:
            stage[name][row * BLOCK : row * BLOCK + BLOCK, :] = block(1 - c, row)
        to_mate(name)
        for row in two:
            acc[name][row, 0:BLOCK, :] = block(c, row)
            acc[name][row, BLOCK:ROWS, :] = jnp.zeros((ROWS - BLOCK, n), jnp.bfloat16)
    g_copy = send(
        g_midt.at[pl.ds(aligned((1 - r) * BLOCK, 16), BLOCK)], g_tok_ref.at[:, mine], end_send.at[1],
        end_recv.at[1], row_mate,
    )
    g_tok_ref[:, mine] = g_midt[pl.ds(aligned(r * BLOCK, 16), BLOCK), :]
    for name in TAIL:
        advance(name)
    while any(level_of[name] < 9 for name in NAMES):
        for name in ORDER:
            if level_of[name] < 9:
                advance(name)
    out_copy.wait()
    g_copy.wait()
    for name in NAMES[2:]:
        mates[name].wait_send()
    release(0)
    release(1)


def run_layer(weights, tokens, cotangent, w_query, w_key_t, w_value_t, lengths, gain_one, gain_two):
    bf, f32 = jnp.bfloat16, jnp.float32
    dma = pltpu.SemaphoreType.DMA
    hbm, vmem = pl.BlockSpec(memory_space=pl.ANY), pl.BlockSpec(memory_space=pltpu.VMEM)
    place = {"x": 0, "y": 0, "z": 0, "c": 0}

    def v(shape, dtype=bf):
        return pltpu.VMEM(shape, dtype)

    scratch = [v((2, 2 * BLOCK, QKV))] + [v((2, 2 * BLOCK, w.shape[1])) for w in weights]
    scratch += [v((2, ROWS, N_OF[name])) for name in OWN_SPACE]
    scratch += [v((2, BLOCK, n) if name[:4] == "down" else (2 * BLOCK, n)) for name, n, _ in STREAMS]
    for _, n, order in STREAMS:
        for level in range(3):
            scratch.append(v((3,) + Stream(order, place).shape(level, n) if level else (6, 128, n)))
    scratch += [
        v((8, 128), jnp.int32), v((8, 128), jnp.int32), v((2, 8, 512), f32), v((2, BLOCK, 128)),
        v((2, BLOCK, 128), f32), v((D, 128)), v((128, D)), v((1600, 128), f32), v((320, 384)),
        v((320, 128)), v((320, 128)), v((KVH, 128, 384), f32), v((D, 128)), v((D, 128), f32),
        v((D, 128)), v((2, 128, 1280), f32), v((2, 128, 1280), f32), v((2, 128, 1280)),
        v((D, 128)), v((2, 128, 1280)), v((2, 128, 1280)),
        v((D, 128), f32), v((992, 128)), v((2, 128, 512)), v((D, 128)), v((2, QKV, 128)), v((D, 128), f32),
        v((8, 128), f32), v((BLOCK, 128), f32), v((BLOCK, 128)), v((BLOCK, 128)), v((8, 128), jnp.int32),
        v((8, 512), f32),
    ]
    scratch += [
        dma((9,)), dma((5, 4)), dma((5, 4)), dma((5, 7)), dma((5, 7)), dma((5, 2)), dma((5, 2)),
        dma((4,)), dma((4,)), dma((9,)), dma((9,)), dma((9, 2, 3)), dma((9, 2, 3)), dma((9,)), dma((2,)), dma((2,)),
        dma((9, 6)), dma((9, 6)), dma((9, 2, 2)),
    ]
    return pl.pallas_call(
        mega_kernel,
        out_shape=[jax.ShapeDtypeStruct((BLOCK, 256), f32)] * 2
        + [jax.ShapeDtypeStruct((ROWS, n), bf) for _, n, _ in STREAMS],
        in_specs=[hbm] * 6 + [vmem] * 6,
        out_specs=[vmem] * 2 + [hbm] * 9,
        scratch_shapes=scratch,
        compiler_params=pltpu.CompilerParams(
            collective_id=1, has_side_effects=True, vmem_limit_bytes=63 * MIB
        ),
        cost_estimate=pl.CostEstimate(flops=8 * 10**9, bytes_accessed=60 * MIB, transcendentals=0),
    )(*weights, tokens, cotangent, w_query, w_key_t, w_value_t, lengths, gain_one, gain_two)


def widen_kernel(
    down0, down1, gate0, gate1, up0, up1, out, q, kv, y, g,
    o_down, o_gate, o_up, o_out, o_q, o_k, o_v, o_one, o_two, o_y, o_g
):
    for a, b, whole in ((down0, down1, o_down), (gate0, gate1, o_gate), (up0, up1, o_up)):
        whole[:, 0:640] = a[...].astype(jnp.float32)
        whole[:, 640:1280] = b[...].astype(jnp.float32)
    o_y[...] = y[...]
    o_g[...] = g[...]
    for a, b in ((out, o_out), (q, o_q)):
        b[...] = a[:, 0:480].astype(jnp.float32)
    flipped = kv[...].astype(jnp.float32).T
    o_k[...] = flipped[0:160]
    o_v[...] = flipped[160:320]
    o_one[...] = flipped[320:321]
    o_two[...] = flipped[321:322]


def widen(sums, out, g_tok):
    f32 = jnp.float32

    def rows(n):
        return pl.BlockSpec((128, n), lambda i: (i, 0))

    def lanes(n):
        return pl.BlockSpec((n, 128), lambda i: (0, i))

    shapes = [(BLOCK, 1280)] * 3 + [(BLOCK, 480)] * 2 + [(160, BLOCK)] * 2 + [(1, BLOCK)] * 2 + [(BLOCK, 256)] * 2
    return pl.pallas_call(
        widen_kernel,
        grid=(4,),
        out_shape=[jax.ShapeDtypeStruct(s, f32) for s in shapes],
        in_specs=[rows(n) for _, n, _ in STREAMS] + [rows(256)] * 2,
        out_specs=[rows(s[1]) for s in shapes[:5]] + [lanes(160)] * 2 + [lanes(1)] * 2 + [rows(256)] * 2,
        compiler_params=pltpu.CompilerParams(vmem_limit_bytes=60 * MIB),
        cost_estimate=pl.CostEstimate(flops=0, bytes_accessed=16 * MIB, transcendentals=0),
    )(*sums, out, g_tok)


def on_device(
    tokens, gain_attn, gain_mlp, w_query, w_key, w_value, w_out, w_gate, w_up, w_down, seq_lengths, cotangent
):
    out, g_tok, *sums = run_layer(
        [w_out, w_gate, w_up, w_down], tokens, cotangent, w_query, w_key.T, w_value.T, seq_lengths,
        gain_attn.reshape(1, BLOCK), gain_mlp.reshape(1, BLOCK),
    )
    down, gate, up, g_out, query, key, value, one, two, out, g_tok = widen(sums, out, g_tok)
    return (
        out, g_tok, one.reshape(BLOCK), two.reshape(BLOCK), query, key.T, value.T, g_out, gate, up, down
    )

def solution(mesh):
    in_specs = (
        P("row", ("tok", "col")), P("row"), P("row"), P("row", "col"), P("row", "col"), P("row", "col"),
        P("col", "row"), P("row", "col"), P("row", "col"), P("row", "col"),
        P(("tok", "row", "col"), None), P("row", ("tok", "col")),
    )
    out_specs = (
        P("row", ("tok", "col")), P("row", ("tok", "col")), P("row"), P("row"), P("row", "col"),
        P("row", "col"), P("row", "col"), P("col", "row"), P("row", "col"), P("row", "col"), P("row", "col"),
    )
    return jax.shard_map(
        on_device, mesh=mesh, in_specs=in_specs, out_specs=out_specs, check_vma=False
    )
```
